32 devices in a mesh: sweep: 2 (over y), tm: 8 (over z, x), unit: 2 (over core).
Axes of the slice: x: 2, y: 2, z: 4, core: 2. Of those that a mesh axis runs over, the one named last changes fastest.
Arguments:
- projections: bfloat16 [2, 32, 3, 1024], P('sweep', 'tm', None, 'unit'), parts along dimension 0, may hold values from -6 to 6
- recurrent: bfloat16 [2048, 3, 1024], P('sweep', None, 'unit'), parts along dimension 0, may hold values from -0.375 to 0.375
- update_bias: float32 [2048], P(('sweep', 'unit')), parts along dimension 0, may hold values from -1 to 13
- candidate_bias: float32 [2048], P(('sweep', 'unit')), parts along dimension 0, may hold values from -5 to 5
- start_state: float32 [2, 1024], P('sweep', 'unit'), parts along dimension 0, may hold values from -4 to 4
- initial_guess: float32 [2, 32, 1024], P('sweep', 'tm', 'unit'), parts along dimension 0, may hold values from -3 to 3
Outputs:
- trajectory: float32 [2, 32, 1024], P('sweep', 'tm', 'unit'), parts along dimension 0
The draws below stay inside these ranges and needn't reach their ends.
There are 2 independent parts, one for each index of `sweep`. The reference program is written for one: setup_inputs(seed, part) draws one part's arguments, and reference() takes and returns one part's arrays. A program takes and returns all parts, laid end to end along the dimension named above; each array names one. Nothing has to cross between parts.
All inputs are finite; a program needn't handle non-finite values.
Results may differ from the reference program's by a relative error of at most 0.0017.
Values may be sent and summed in bfloat16 or wider, within the bound.
A program may use at most 64 MiB of HBM per device.

```python
import jax
import jax.numpy as jnp
from jax import lax

H = 1024
BLOCK = 128
BATCH = 1
NEWTON = 2
LENGTH = 32


def draw_update_bias(key, part):
    first_key = jax.random.fold_in(key, 11)
    second_key = jax.random.fold_in(key, 23)
    third_key = jax.random.fold_in(key, 37)
    quick_bias = jax.random.uniform(first_key, (H,), jnp.float32, -1.0, 4.0)
    slow_bias = jax.random.uniform(second_key, (H,), jnp.float32, 10.0, 13.0)
    slow_share = 0.25
    chosen = jax.random.uniform(third_key, (H,), jnp.float32) < slow_share
    return jnp.where(chosen, slow_bias, quick_bias).astype(jnp.float32)


def block_levels(key, shape, cuts, low, high):
    gain = 1.0
    for dim, shards_of in cuts:
        heights = jax.random.uniform(jax.random.fold_in(jax.random.fold_in(key, 6), dim), (shards_of,), jnp.float32, low / len(cuts), high / len(cuts))
        gain = gain * jnp.repeat(jnp.exp(heights), shape[dim] // shards_of).reshape((-1,) + (1,) * (len(shape) - 1 - dim))
    return gain


def scatter_about(key, extent, scale, limit, split=(), kind=jnp.bfloat16):
    values = scale * jax.random.normal(key, extent, jnp.float32)
    if split:
        values = values * block_levels(key, extent, split, -0.22, 0.18)
    return jnp.clip(values, -limit, limit).astype(kind)


def setup_inputs(seed: int = 0, part: int = 0) -> dict:
    key_of = jax.random.split(jax.random.key(seed), 7)
    own_keys = jax.random.split(jax.random.fold_in(key_of[6], part), 7)
    projections = scatter_about(own_keys[0], (BATCH, LENGTH, 3, H), 1.0, 6.0, ((1, 8), (3, 2)))
    recurrent = scatter_about(own_keys[1], (H, 3, H), (H // 4) ** -0.5, 0.375, ((2, 2),))
    update_bias = draw_update_bias(jax.random.fold_in(jax.random.fold_in(key_of[6], part), 71), part)
    candidate_bias = scatter_about(own_keys[3], (H,), 1.0, 5.0, ((0, 2),), jnp.float32)
    start_state = scatter_about(own_keys[4], (BATCH, H), 0.7, 4.0, ((1, 2),), jnp.float32)
    initial_guess = scatter_about(own_keys[5], (BATCH, LENGTH, H), 0.5, 3.0, ((1, 8), (2, 2)), jnp.float32)
    return {"projections": projections, "recurrent": recurrent, "update_bias": update_bias, "candidate_bias": candidate_bias, "start_state": start_state, "initial_guess": initial_guess}


def jacobian_apply(vector, update_gate, coef_a, coef_c, coef_d, blocks):
    lead_shape = vector.shape[:-1]
    grouped = vector.reshape(lead_shape + (H // BLOCK, BLOCK))
    block_terms = jnp.einsum("...ki,kigj->...gkj", grouped, blocks, precision=lax.Precision.HIGHEST)
    block_terms = block_terms.reshape(lead_shape + (3, H))
    return (update_gate * vector + coef_a * block_terms[..., 0, :]
            + coef_c * block_terms[..., 1, :] + coef_d * block_terms[..., 2, :])


def reference(projections, recurrent, update_bias, candidate_bias, start_state, initial_guess):
    blocks = recurrent.astype(jnp.float32).reshape(H // BLOCK, BLOCK, 3, H // BLOCK, BLOCK)
    blocks = jnp.einsum("kigkj->kigj", blocks)
    flat_weight = recurrent.reshape(H, 3 * H)
    trajectory = initial_guess
    for newton_turn in range(NEWTON):
        previous = jnp.concatenate([start_state[:, None, :], trajectory[:, :-1, :]], axis=1)
        panels = previous.astype(jnp.bfloat16).reshape(BATCH * LENGTH, H)
        recurrent_terms = jnp.dot(panels, flat_weight, preferred_element_type=jnp.float32)
        recurrent_terms = recurrent_terms.reshape(BATCH, LENGTH, 3, H)
        update_gate = jax.nn.sigmoid(projections[:, :, 0].astype(jnp.float32) + recurrent_terms[:, :, 0] + update_bias)
        reset_gate = jax.nn.sigmoid(projections[:, :, 1].astype(jnp.float32) + recurrent_terms[:, :, 1])
        cand_rec = recurrent_terms[:, :, 2] + candidate_bias
        candidate = jnp.tanh(projections[:, :, 2].astype(jnp.float32) + reset_gate * cand_rec)
        mapped = (1.0 - update_gate) * candidate + update_gate * previous
        coef_a = (previous - candidate) * update_gate * (1.0 - update_gate)
        coef_d = (1.0 - update_gate) * (1.0 - candidate * candidate) * reset_gate
        coef_c = coef_d * cand_rec * (1.0 - reset_gate)
        offsets = mapped - jacobian_apply(previous, update_gate, coef_a, coef_c, coef_d, blocks)

        def advance(current, inputs):
            gate_step, a_step, c_step, d_step, offset_step = inputs
            following = jacobian_apply(current, gate_step, a_step, c_step, d_step, blocks) + offset_step
            return following, following

        sequence_inputs = tuple(jnp.transpose(item, (1, 0, 2)) for item in (update_gate, coef_a, coef_c, coef_d, offsets))
        carried, states = lax.scan(advance, start_state, sequence_inputs)
        trajectory = jnp.transpose(states, (1, 0, 2))
    return trajectory
```

```python
import functools

import jax
import jax.numpy as jnp
from jax import lax
from jax.experimental import pallas as pl
from jax.experimental.pallas import tpu as pltpu
from jax.sharding import PartitionSpec as P

BLOCK = 128
NEWTON = 2
GROUP = 8
COEFS = 5
FINE = (0, 4)
SENT = COEFS + len(FINE)
MESH = pl.DeviceIdType.MESH


def to(tm, unit):
    return {"tm": tm, "unit": unit}


def newton_kernel(
    n_tm, n_unit, proj, w_hbm, bias_u, bias_c, start, guess_in, out,
    w_all, w_diag, stage, mates, nears, own, packed, coefs, moves, relay_out, relay_in,
    w_sem, mate_send, mate_recv, near_send, near_recv, coef_send, coef_recv, relay_send, relay_recv,
):
    steps, width = guess_in.shape
    blocks = width // BLOCK
    rows = steps * blocks
    group = min(GROUP, n_tm)
    n_groups = n_tm // group
    time = lax.axis_index("tm")
    unit = lax.axis_index("unit")
    place = lax.rem(time, group)
    reach = min(n_tm - 1, group if n_groups > 1 else group - 1)

    loads = [
        pltpu.make_async_copy(w_hbm.at[gate], w_all.at[gate], w_sem.at[gate]) for gate in range(3)
    ]
    for load in loads:
        load.start()

    barrier = pltpu.get_barrier_semaphore()
    greeted = jnp.int32(n_unit - 1)
    for away in range(1, n_unit):
        pl.semaphore_signal(
            barrier, inc=1, device_id=to(time, lax.rem(unit + away, n_unit)), device_id_type=MESH
        )
    for away in range(1, reach + 1):
        turns = range(n_unit if away == 1 else 1)
        for there, valid in ((time + away, time + away < n_tm), (time - away, time >= away)):
            greeted = greeted + jnp.where(valid, len(turns), 0)

            @pl.when(valid)
            def _():
                for turn in turns:
                    pl.semaphore_signal(
                        barrier, inc=1, device_id=to(there, lax.rem(unit + turn, n_unit)), device_id_type=MESH
                    )

    stage[0, 0:steps, :] = guess_in[...]
    stage[0, steps : steps + 1, :] = start[...]
    pl.semaphore_wait(barrier, greeted)

    def mate_copy(turn, away):
        return pltpu.make_async_remote_copy(
            src_ref=stage.at[turn], dst_ref=mates.at[turn, away - 1],
            send_sem=mate_send.at[turn, away - 1], recv_sem=mate_recv.at[turn, away - 1],
            device_id=to(time, lax.rem(unit + away, n_unit)), device_id_type=MESH,
        )

    def near_copy(away):
        return pltpu.make_async_remote_copy(
            src_ref=stage.at[0], dst_ref=nears.at[away],
            send_sem=near_send.at[away], recv_sem=near_recv.at[away],
            device_id=to(lax.rem(time + 1, n_tm), lax.rem(unit + away, n_unit)), device_id_type=MESH,
        )

    def coef_copy(turn, away):
        return pltpu.make_async_remote_copy(
            src_ref=packed.at[turn], dst_ref=coefs.at[turn, away - 1],
            send_sem=coef_send.at[turn, away - 1], recv_sem=coef_recv.at[turn, away - 1],
            device_id=to(lax.rem(time + away, n_tm), unit), device_id_type=MESH,
        )

    def relay_copy(turn, target):
        return pltpu.make_async_remote_copy(
            src_ref=relay_out.at[turn], dst_ref=relay_in.at[turn],
            send_sem=relay_send.at[turn, target], recv_sem=relay_recv.at[turn],
            device_id=to(lax.rem(time + 1 + target, n_tm), unit), device_id_type=MESH,
        )

    for away in range(1, n_unit):
        mate_copy(0, away).start()

    @pl.when(time < n_tm - 1)
    def _():
        for away in range(n_unit):
            near_copy(away).start()

    @pl.when(time > 0)
    def _():
        for away in range(n_unit):
            near_copy(away).wait_recv()

    def entering_from(held, away):
        return jnp.where(time == 0, held[steps : steps + 1, :], nears[(n_unit - away) % n_unit, steps - 1 : steps, :])

    guess = guess_in[...]
    previous = jnp.concatenate([entering_from(stage[0], 0), guess[: steps - 1]], axis=0)
    row = lax.broadcasted_iota(jnp.int32, (16, BLOCK), 0) % 8

    for turn in range(NEWTON):
        if turn:
            stage[turn, 0:steps, :] = previous
            for away in range(1, n_unit):
                mate_copy(turn, away).start()

        if turn == 0:
            for load in loads:
                load.wait()
            for block in range(blocks):
                first = pl.multiple_of(unit * width + block * BLOCK, BLOCK)
                here = slice(block * BLOCK, (block + 1) * BLOCK)
                for gate in range(3):
                    w_diag[here, gate * BLOCK : (gate + 1) * BLOCK] = w_all[gate, pl.ds(first, BLOCK), here]

        def product(panel, owner):
            first = pl.multiple_of(owner * width, width)
            panel = jnp.concatenate([panel] * (16 // steps), axis=0).astype(jnp.bfloat16)
            return [
                jnp.dot(panel, w_all[gate, pl.ds(first, width), :], preferred_element_type=jnp.float32)[:steps]
                for gate in range(3)
            ]

        rec = product(previous, unit)
        for away in range(1, n_unit):
            mate_copy(turn, away).wait_recv()
            held = mates[turn, away - 1]
            if turn:
                panel = held[:steps]
            else:
                panel = jnp.concatenate([entering_from(held, n_unit - away), held[: steps - 1]], axis=0)
            rec = [x + y for x, y in zip(rec, product(panel, lax.rem(unit + n_unit - away, n_unit)))]

        update_in = proj[0].astype(jnp.float32) + rec[0] + bias_u[...]
        update = jax.nn.sigmoid(update_in)
        fresh = jax.nn.sigmoid(-update_in)
        reset = jax.nn.sigmoid(proj[1].astype(jnp.float32) + rec[1])
        cand_rec = rec[2] + bias_c[...]
        cand = jnp.tanh(proj[2].astype(jnp.float32) + reset * cand_rec)
        coef_d = fresh * (1.0 - cand * cand) * reset
        values = (
            fresh,
            (previous - cand) * update * fresh,
            coef_d * cand_rec * (1.0 - reset),
            coef_d,
            fresh * cand + update * previous - guess,
        )
        for index, value in enumerate(values):
            for block in range(blocks):
                own[index, pl.ds(block, steps, stride=blocks), :] = value[:, block * BLOCK : (block + 1) * BLOCK]
        packed[turn, 0:COEFS] = own[...].astype(jnp.bfloat16)
        for slot, index in enumerate(FINE):
            full = own[index]
            packed[turn, COEFS + slot] = (full - full.astype(jnp.bfloat16).astype(jnp.float32)).astype(jnp.bfloat16)

        for away in range(group - 1, 0, -1):
            @pl.when(place + away < group)
            def _():
                coef_copy(turn, away).start()

        def step(delta, five):
            high = delta.astype(jnp.bfloat16).astype(jnp.float32)
            both = jnp.concatenate([high, delta - high], axis=0)
            left = jnp.concatenate(
                [jnp.where(row == block, both, 0.0) for block in range(blocks)], axis=1
            ).astype(jnp.bfloat16)
            terms = jnp.dot(left, w_diag[...], preferred_element_type=jnp.float32)
            terms = terms[:8] + terms[8:]
            fresh, a, c, d, gap = five
            return (
                (gap + delta - fresh * delta) + a * terms[:, :BLOCK]
                + c * terms[:, BLOCK : 2 * BLOCK] + d * terms[:, 2 * BLOCK :]
            )

        def at_step(table, t):
            def pick(value):
                part = value[t * blocks : (t + 1) * blocks]
                return jnp.concatenate([part] * (8 // blocks), axis=0)

            return [pick(table[index]) for index in range(COEFS)]

        def pass_block(source, delta):
            away = place - source
            slot = away - 1
            pltpu.make_async_remote_copy(
                src_ref=packed.at[turn], dst_ref=coefs.at[turn, slot],
                send_sem=coef_send.at[turn, slot], recv_sem=coef_recv.at[turn, slot],
                device_id=to(lax.rem(time + 1, n_tm), unit), device_id_type=MESH,
            ).wait_recv()
            table = [coefs[turn, slot, index].astype(jnp.float32) for index in range(SENT)]
            for low, index in enumerate(FINE):
                table[index] = table[index] + table[COEFS + low]
            for t in range(steps):
                delta = step(delta, at_step(table, t))
            return delta

        delta = jnp.zeros((8, BLOCK), jnp.float32)
        if n_groups > 1:
            relay_in_now = relay_in.at[turn]

            @pl.when(time < group)
            def _():
                relay_in_now[...] = jnp.zeros((8, BLOCK), jnp.float32)

            @pl.when(time >= group)
            def _():
                relay_copy(turn, 0).wait_recv()

            delta = relay_in_now[...]
        delta = lax.fori_loop(0, place, pass_block, delta)
        moves[0:blocks, :] = delta[:blocks]
        table = own[...]
        for t in range(steps):
            delta = step(delta, at_step(table, t))
            moves[(t + 1) * blocks : (t + 2) * blocks, :] = delta[:blocks]
        if n_groups > 1:
            relay_out[turn] = delta

            @pl.when((place == group - 1) & (time < n_tm - 1))
            def _():
                for target in range(group):
                    relay_copy(turn, target).start()

        def moved(skip):
            return jnp.concatenate(
                [moves[pl.ds(skip * blocks + block, steps, stride=blocks), :] for block in range(blocks)], axis=1
            )

        guess = guess + moved(1)
        if turn < NEWTON - 1:
            previous = previous + moved(0)
    out[...] = guess

    @pl.when(time < n_tm - 1)
    def _():
        for away in range(n_unit):
            near_copy(away).wait_send()

    for turn in range(NEWTON):
        for away in range(1, n_unit):
            mate_copy(turn, away).wait_send()
        for away in range(1, group):
            @pl.when(place + away < group)
            def _():
                coef_copy(turn, away).wait_send()
        if n_groups > 1:
            @pl.when((place == group - 1) & (time < n_tm - 1))
            def _():
                for target in range(group):
                    relay_copy(turn, target).wait_send()


def shards(n_tm, n_unit, projections, recurrent, update_bias, candidate_bias, start_state, initial_guess):
    _, steps, _, width = projections.shape
    full = recurrent.shape[0]
    rows = steps * (width // BLOCK)
    group = min(GROUP, n_tm)
    vmem = pl.BlockSpec(memory_space=pltpu.VMEM)
    f32, bf16 = jnp.float32, jnp.bfloat16
    held = 8 * pl.cdiv(steps + 1, 8)
    dma = pltpu.SemaphoreType.DMA
    result = pl.pallas_call(
        functools.partial(newton_kernel, n_tm, n_unit),
        out_shape=jax.ShapeDtypeStruct((steps, width), f32),
        in_specs=[vmem, pl.BlockSpec(memory_space=pl.ANY), vmem, vmem, vmem, vmem],
        out_specs=vmem,
        scratch_shapes=[
            pltpu.VMEM((3, full, width), bf16),
            pltpu.VMEM((width, 3 * BLOCK), bf16),
            pltpu.VMEM((NEWTON, held, width), f32),
            pltpu.VMEM((NEWTON, n_unit - 1, held, width), f32),
            pltpu.VMEM((n_unit, held, width), f32),
            pltpu.VMEM((COEFS, rows, BLOCK), f32),
            pltpu.VMEM((NEWTON, SENT, rows, BLOCK), bf16),
            pltpu.VMEM((NEWTON, group - 1, SENT, rows, BLOCK), bf16),
            pltpu.VMEM((rows + 8, BLOCK), f32),
            pltpu.VMEM((NEWTON, 8, BLOCK), f32),
            pltpu.VMEM((NEWTON, 8, BLOCK), f32),
            dma((3,)),
            dma((NEWTON, n_unit - 1)),
            dma((NEWTON, n_unit - 1)),
            dma((n_unit,)),
            dma((n_unit,)),
            dma((NEWTON, group - 1)),
            dma((NEWTON, group - 1)),
            dma((NEWTON, group)),
            dma((NEWTON,)),
        ],
        compiler_params=pltpu.CompilerParams(
            collective_id=0, has_side_effects=True, vmem_limit_bytes=32 * 1024 * 1024
        ),
        name="newton",
    )(
        jnp.transpose(projections[0], (1, 0, 2)),
        jnp.transpose(recurrent, (1, 0, 2)),
        update_bias.reshape(1, width),
        candidate_bias.reshape(1, width),
        start_state,
        initial_guess[0],
    )
    return result[None]


def solution(mesh):
    return jax.shard_map(
        functools.partial(shards, mesh.shape["tm"], mesh.shape["unit"]),
        mesh=mesh,
        in_specs=(
            P("sweep", "tm", None, "unit"),
            P("sweep", None, "unit"),
            P(("sweep", "unit")),
            P(("sweep", "unit")),
            P("sweep", "unit"),
            P("sweep", "tm", "unit"),
        ),
        out_specs=P("sweep", "tm", "unit"),
        check_vma=False,
    )
```

```python
import functools

import jax
import jax.numpy as jnp
from jax import lax
from jax.experimental import pallas as pl
from jax.experimental.pallas import tpu as pltpu
from jax.sharding import PartitionSpec as P

BLOCK = 128
NEWTON = 2
GROUP = 8
COEFS = 5
FINE = (0, 4)
SENT = COEFS + len(FINE)
MESH = pl.DeviceIdType.MESH


def to(tm, unit):
    return {"tm": tm, "unit": unit}


def newton_kernel(
    n_tm, n_unit, proj_hbm, w_hbm, bias_u_hbm, bias_c_hbm, start_hbm, guess_hbm, out,
    proj, bias_u, bias_c, w_all, w_diag, stage, mates, nears, own, packed, coefs, moves, relay_out, relay_in,
    in_sem, w_sem, mate_send, mate_recv, near_send, near_recv, coef_send, coef_recv, relay_send, relay_recv,
):
    steps, width = guess_hbm.shape
    blocks = width // BLOCK
    rows = steps * blocks
    group = min(GROUP, n_tm)
    n_groups = n_tm // group
    time = lax.axis_index("tm")
    unit = lax.axis_index("unit")
    place = lax.rem(time, group)
    reach = min(n_tm - 1, group if n_groups > 1 else group - 1)

    smalls = [
        pltpu.make_async_copy(source, target, in_sem.at[index])
        for index, (source, target) in enumerate((
            (guess_hbm, stage.at[0, pl.ds(0, steps)]),
            (start_hbm, stage.at[0, pl.ds(steps, 1)]),
            (proj_hbm, proj),
            (bias_u_hbm, bias_u),
            (bias_c_hbm, bias_c),
        ))
    ]
    for load in smalls:
        load.start()
    loads = [
        pltpu.make_async_copy(w_hbm.at[gate], w_all.at[gate], w_sem.at[gate]) for gate in range(3)
    ]
    for load in loads:
        load.start()

    barrier = pltpu.get_barrier_semaphore()
    greeted = jnp.int32(n_unit - 1)
    for away in range(1, n_unit):
        pl.semaphore_signal(
            barrier, inc=1, device_id=to(time, lax.rem(unit + away, n_unit)), device_id_type=MESH
        )
    for away in range(1, reach + 1):
        turns = range(n_unit if away == 1 else 1)
        for there, valid in ((time + away, time + away < n_tm), (time - away, time >= away)):
            greeted = greeted + jnp.where(valid, len(turns), 0)

            @pl.when(valid)
            def _():
                for turn in turns:
                    pl.semaphore_signal(
                        barrier, inc=1, device_id=to(there, lax.rem(unit + turn, n_unit)), device_id_type=MESH
                    )

    for load in smalls[:2]:
        load.wait()
    pl.semaphore_wait(barrier, greeted)

    def mate_copy(turn, away):
        return pltpu.make_async_remote_copy(
            src_ref=stage.at[turn], dst_ref=mates.at[turn, away - 1],
            send_sem=mate_send.at[turn, away - 1], recv_sem=mate_recv.at[turn, away - 1],
            device_id=to(time, lax.rem(unit + away, n_unit)), device_id_type=MESH,
        )

    def near_copy(away):
        return pltpu.make_async_remote_copy(
            src_ref=stage.at[0], dst_ref=nears.at[away],
            send_sem=near_send.at[away], recv_sem=near_recv.at[away],
            device_id=to(lax.rem(time + 1, n_tm), lax.rem(unit + away, n_unit)), device_id_type=MESH,
        )

    def coef_copy(turn, away):
        return pltpu.make_async_remote_copy(
            src_ref=packed.at[turn], dst_ref=coefs.at[turn, away - 1],
            send_sem=coef_send.at[turn, away - 1], recv_sem=coef_recv.at[turn, away - 1],
            device_id=to(lax.rem(time + away, n_tm), unit), device_id_type=MESH,
        )

    def relay_copy(turn, target):
        return pltpu.make_async_remote_copy(
            src_ref=relay_out.at[turn], dst_ref=relay_in.at[turn],
            send_sem=relay_send.at[turn, target], recv_sem=relay_recv.at[turn],
            device_id=to(lax.rem(time + 1 + target, n_tm), unit), device_id_type=MESH,
        )

    for away in range(1, n_unit):
        mate_copy(0, away).start()

    @pl.when(time < n_tm - 1)
    def _():
        for away in range(n_unit):
            near_copy(away).start()

    @pl.when(time > 0)
    def _():
        for away in range(n_unit):
            near_copy(away).wait_recv()

    def entering_from(held, away):
        return jnp.where(time == 0, held[steps : steps + 1, :], nears[(n_unit - away) % n_unit, steps - 1 : steps, :])

    guess = stage[0, 0:steps, :]
    previous = jnp.concatenate([entering_from(stage[0], 0), guess[: steps - 1]], axis=0)
    row = lax.broadcasted_iota(jnp.int32, (16, BLOCK), 0) % 8

    for turn in range(NEWTON):
        if turn:
            stage[turn, 0:steps, :] = previous
            for away in range(1, n_unit):
                mate_copy(turn, away).start()

        if turn == 0:
            for load in loads:
                load.wait()
            for load in smalls[2:]:
                load.wait()
            for block in range(blocks):
                first = pl.multiple_of(unit * width + block * BLOCK, BLOCK)
                here = slice(block * BLOCK, (block + 1) * BLOCK)
                for gate in range(3):
                    w_diag[here, gate * BLOCK : (gate + 1) * BLOCK] = w_all[gate, pl.ds(first, BLOCK), here]

        def product(panel, owner):
            first = pl.multiple_of(owner * width, width)
            panel = jnp.concatenate([panel] * (16 // steps), axis=0).astype(jnp.bfloat16)
            return [
                jnp.dot(panel, w_all[gate, pl.ds(first, width), :], preferred_element_type=jnp.float32)[:steps]
                for gate in range(3)
            ]

        rec = product(previous, unit)
        for away in range(1, n_unit):
            mate_copy(turn, away).wait_recv()
            held = mates[turn, away - 1]
            if turn:
                panel = held[:steps]
            else:
                panel = jnp.concatenate([entering_from(held, n_unit - away), held[: steps - 1]], axis=0)
            rec = [x + y for x, y in zip(rec, product(panel, lax.rem(unit + n_unit - away, n_unit)))]

        update_in = proj[0].astype(jnp.float32) + rec[0] + bias_u[...]
        update = jax.nn.sigmoid(update_in)
        fresh = jax.nn.sigmoid(-update_in)
        reset = jax.nn.sigmoid(proj[1].astype(jnp.float32) + rec[1])
        cand_rec = rec[2] + bias_c[...]
        cand = jnp.tanh(proj[2].astype(jnp.float32) + reset * cand_rec)
        coef_d = fresh * (1.0 - cand * cand) * reset
        values = (
            fresh,
            (previous - cand) * update * fresh,
            coef_d * cand_rec * (1.0 - reset),
            coef_d,
            fresh * cand + update * previous - guess,
        )
        for index, value in enumerate(values):
            for block in range(blocks):
                own[index, pl.ds(block, steps, stride=blocks), :] = value[:, block * BLOCK : (block + 1) * BLOCK]
        packed[turn, 0:COEFS] = own[...].astype(jnp.bfloat16)
        for slot, index in enumerate(FINE):
            full = own[index]
            packed[turn, COEFS + slot] = (full - full.astype(jnp.bfloat16).astype(jnp.float32)).astype(jnp.bfloat16)

        for away in range(group - 1, 0, -1):
            @pl.when(place + away < group)
            def _():
                coef_copy(turn, away).start()

        def step(delta, five):
            high = delta.astype(jnp.bfloat16).astype(jnp.float32)
            both = jnp.concatenate([high, delta - high], axis=0)
            left = jnp.concatenate(
                [jnp.where(row == block, both, 0.0) for block in range(blocks)], axis=1
            ).astype(jnp.bfloat16)
            terms = jnp.dot(left, w_diag[...], preferred_element_type=jnp.float32)
            terms = terms[:8] + terms[8:]
            fresh, a, c, d, gap = five
            return (
                (gap + delta - fresh * delta) + a * terms[:, :BLOCK]
                + c * terms[:, BLOCK : 2 * BLOCK] + d * terms[:, 2 * BLOCK :]
            )

        def at_step(table, t):
            def pick(value):
                part = value[t * blocks : (t + 1) * blocks]
                return jnp.concatenate([part] * (8 // blocks), axis=0)

            return [pick(table[index]) for index in range(COEFS)]

        def pass_block(source, delta):
            away = place - source
            slot = away - 1
            pltpu.make_async_remote_copy(
                src_ref=packed.at[turn], dst_ref=coefs.at[turn, slot],
                send_sem=coef_send.at[turn, slot], recv_sem=coef_recv.at[turn, slot],
                device_id=to(lax.rem(time + 1, n_tm), unit), device_id_type=MESH,
            ).wait_recv()
            table = [coefs[turn, slot, index].astype(jnp.float32) for index in range(SENT)]
            for low, index in enumerate(FINE):
                table[index] = table[index] + table[COEFS + low]
            for t in range(steps):
                delta = step(delta, at_step(table, t))
            return delta

        delta = jnp.zeros((8, BLOCK), jnp.float32)
        if n_groups > 1:
            relay_in_now = relay_in.at[turn]

            @pl.when(time < group)
            def _():
                relay_in_now[...] = jnp.zeros((8, BLOCK), jnp.float32)

            @pl.when(time >= group)
            def _():
                relay_copy(turn, 0).wait_recv()

            delta = relay_in_now[...]
        delta = lax.fori_loop(0, place, pass_block, delta)
        moves[0:blocks, :] = delta[:blocks]
        table = own[...]
        for t in range(steps):
            delta = step(delta, at_step(table, t))
            moves[(t + 1) * blocks : (t + 2) * blocks, :] = delta[:blocks]
        if n_groups > 1:
            relay_out[turn] = delta

            @pl.when((place == group - 1) & (time < n_tm - 1))
            def _():
                for target in range(group):
                    relay_copy(turn, target).start()

        def moved(skip):
            return jnp.concatenate(
                [moves[pl.ds(skip * blocks + block, steps, stride=blocks), :] for block in range(blocks)], axis=1
            )

        guess = guess + moved(1)
        if turn < NEWTON - 1:
            previous = previous + moved(0)
    out[...] = guess

    @pl.when(time < n_tm - 1)
    def _():
        for away in range(n_unit):
            near_copy(away).wait_send()

    for turn in range(NEWTON):
        for away in range(1, n_unit):
            mate_copy(turn, away).wait_send()
        for away in range(1, group):
            @pl.when(place + away < group)
            def _():
                coef_copy(turn, away).wait_send()
        if n_groups > 1:
            @pl.when((place == group - 1) & (time < n_tm - 1))
            def _():
                for target in range(group):
                    relay_copy(turn, target).wait_send()


def shards(n_tm, n_unit, projections, recurrent, update_bias, candidate_bias, start_state, initial_guess):
    _, steps, _, width = projections.shape
    full = recurrent.shape[0]
    rows = steps * (width // BLOCK)
    group = min(GROUP, n_tm)
    vmem = pl.BlockSpec(memory_space=pltpu.VMEM)
    f32, bf16 = jnp.float32, jnp.bfloat16
    held = 8 * pl.cdiv(steps + 1, 8)
    dma = pltpu.SemaphoreType.DMA
    result = pl.pallas_call(
        functools.partial(newton_kernel, n_tm, n_unit),
        out_shape=jax.ShapeDtypeStruct((steps, width), f32),
        in_specs=[pl.BlockSpec(memory_space=pltpu.HBM)] * 6,
        out_specs=vmem,
        scratch_shapes=[
            pltpu.VMEM((3, steps, width), bf16),
            pltpu.VMEM((1, width), f32),
            pltpu.VMEM((1, width), f32),
            pltpu.VMEM((3, full, width), bf16),
            pltpu.VMEM((width, 3 * BLOCK), bf16),
            pltpu.VMEM((NEWTON, held, width), f32),
            pltpu.VMEM((NEWTON, n_unit - 1, held, width), f32),
            pltpu.VMEM((n_unit, held, width), f32),
            pltpu.VMEM((COEFS, rows, BLOCK), f32),
            pltpu.VMEM((NEWTON, SENT, rows, BLOCK), bf16),
            pltpu.VMEM((NEWTON, group - 1, SENT, rows, BLOCK), bf16),
            pltpu.VMEM((rows + 8, BLOCK), f32),
            pltpu.VMEM((NEWTON, 8, BLOCK), f32),
            pltpu.VMEM((NEWTON, 8, BLOCK), f32),
            dma((5,)),
            dma((3,)),
            dma((NEWTON, n_unit - 1)),
            dma((NEWTON, n_unit - 1)),
            dma((n_unit,)),
            dma((n_unit,)),
            dma((NEWTON, group - 1)),
            dma((NEWTON, group - 1)),
            dma((NEWTON, group)),
            dma((NEWTON,)),
        ],
        compiler_params=pltpu.CompilerParams(
            collective_id=0, has_side_effects=True, vmem_limit_bytes=60 * 1024 * 1024
        ),
        name="newton",
    )(
        jnp.transpose(projections[0], (1, 0, 2)),
        jnp.transpose(recurrent, (1, 0, 2)),
        update_bias.reshape(1, width),
        candidate_bias.reshape(1, width),
        start_state,
        initial_guess[0],
    )
    return result[None]


def solution(mesh):
    return jax.shard_map(
        functools.partial(shards, mesh.shape["tm"], mesh.shape["unit"]),
        mesh=mesh,
        in_specs=(
            P("sweep", "tm", None, "unit"),
            P("sweep", None, "unit"),
            P(("sweep", "unit")),
            P(("sweep", "unit")),
            P("sweep", "unit"),
            P("sweep", "tm", "unit"),
        ),
        out_specs=P("sweep", "tm", "unit"),
        check_vma=False,
    )
```

```python
import functools
import math

import jax
import jax.numpy as jnp
from jax import lax
from jax.experimental import pallas as pl
from jax.experimental.pallas import tpu as pltpu
from jax.sharding import PartitionSpec as P

BLOCK = 128
NEWTON = 2
GROUP = 8
COEFS = 5
MESH = pl.DeviceIdType.MESH


def to(tm, unit):
    return {"tm": tm, "unit": unit}


def newton_kernel(
    n_tm, n_unit, proj_hbm, w_hbm, bias_u_hbm, bias_c_hbm, start_hbm, guess_hbm, out,
    proj, bias_u, bias_c, w_all, w_diag, stage, mates, nears, own, coefs, found, moves, relay_out, relay_in,
    in_sem, w_sem, mate_send, mate_recv, near_send, near_recv, coef_send, coef_recv, move_send, move_recv, relay_send, relay_recv,
):
    steps, width = guess_hbm.shape
    blocks = width // BLOCK
    group = min(GROUP, n_tm)
    split = math.gcd(blocks, group)
    count = blocks // split
    rows = steps * count
    n_groups = n_tm // group
    time = lax.axis_index("tm")
    unit = lax.axis_index("unit")
    place = lax.rem(time, group)
    column = lax.rem(place, split)
    last_row = place >= group - split
    reach = min(n_tm - 1, group if n_groups > 1 else group - 1)

    smalls = [
        pltpu.make_async_copy(source, target, in_sem.at[index])
        for index, (source, target) in enumerate((
            (guess_hbm, stage.at[0, pl.ds(0, steps)]),
            (start_hbm, stage.at[0, pl.ds(steps, 1)]),
            (proj_hbm, proj),
            (bias_u_hbm, bias_u),
            (bias_c_hbm, bias_c),
        ))
    ]
    for load in smalls:
        load.start()
    loads = [
        pltpu.make_async_copy(w_hbm.at[gate], w_all.at[gate], w_sem.at[gate]) for gate in range(3)
    ]
    for load in loads:
        load.start()

    barrier = pltpu.get_barrier_semaphore()
    greeted = jnp.int32(n_unit - 1)
    for away in range(1, n_unit):
        pl.semaphore_signal(
            barrier, inc=1, device_id=to(time, lax.rem(unit + away, n_unit)), device_id_type=MESH
        )
    for away in range(1, reach + 1):
        turns = range(n_unit if away == 1 else 1)
        for there, valid in ((time + away, time + away < n_tm), (time - away, time >= away)):
            greeted = greeted + jnp.where(valid, len(turns), 0)

            @pl.when(valid)
            def _():
                for turn in turns:
                    pl.semaphore_signal(
                        barrier, inc=1, device_id=to(there, lax.rem(unit + turn, n_unit)), device_id_type=MESH
                    )

    for load in smalls[:2]:
        load.wait()
    pl.semaphore_wait(barrier, greeted)

    def mate_copy(turn, away):
        return pltpu.make_async_remote_copy(
            src_ref=stage.at[turn], dst_ref=mates.at[turn, away - 1],
            send_sem=mate_send.at[turn, away - 1], recv_sem=mate_recv.at[turn, away - 1],
            device_id=to(time, lax.rem(unit + away, n_unit)), device_id_type=MESH,
        )

    def near_copy(away):
        return pltpu.make_async_remote_copy(
            src_ref=stage.at[0], dst_ref=nears.at[away],
            send_sem=near_send.at[away], recv_sem=near_recv.at[away],
            device_id=to(lax.rem(time + 1, n_tm), lax.rem(unit + away, n_unit)), device_id_type=MESH,
        )

    def coef_copy(turn, away):
        return pltpu.make_async_remote_copy(
            src_ref=own.at[turn, lax.rem(place + away + group, split)], dst_ref=coefs.at[turn, place],
            send_sem=coef_send.at[turn, away + split], recv_sem=coef_recv.at[turn, place],
            device_id=to(lax.rem(time + away + n_tm, n_tm), unit), device_id_type=MESH,
        )

    def coef_wanted(away):
        there = place + away
        return (there < group) & (there >= place - column)

    def coef_arrival(turn, source):
        return pltpu.make_async_remote_copy(
            src_ref=own.at[turn, 0], dst_ref=coefs.at[turn, source],
            send_sem=coef_send.at[turn, 0], recv_sem=coef_recv.at[turn, source],
            device_id=to(lax.rem(time + 1, n_tm), unit), device_id_type=MESH,
        )

    def move_copy(turn, member):
        return pltpu.make_async_remote_copy(
            src_ref=found.at[turn, member], dst_ref=moves.at[turn, column],
            send_sem=move_send.at[turn, member], recv_sem=move_recv.at[turn, column],
            device_id=to(time - column + member, unit), device_id_type=MESH,
        )

    def move_arrival(turn, member):
        return pltpu.make_async_remote_copy(
            src_ref=found.at[turn, member], dst_ref=moves.at[turn, member],
            send_sem=move_send.at[turn, member], recv_sem=move_recv.at[turn, member],
            device_id=to(time - column + member, unit), device_id_type=MESH,
        )

    def relay_copy(turn, target):
        return pltpu.make_async_remote_copy(
            src_ref=relay_out.at[turn], dst_ref=relay_in.at[turn],
            send_sem=relay_send.at[turn, target], recv_sem=relay_recv.at[turn],
            device_id=to(lax.rem(time - place + group + target * split + column, n_tm), unit), device_id_type=MESH,
        )

    for away in range(1, n_unit):
        mate_copy(0, away).start()

    @pl.when(time < n_tm - 1)
    def _():
        for away in range(n_unit):
            near_copy(away).start()

    @pl.when(time > 0)
    def _():
        for away in range(n_unit):
            near_copy(away).wait_recv()

    def entering_from(held, away):
        return jnp.where(time == 0, held[steps : steps + 1, :], nears[(n_unit - away) % n_unit, steps - 1 : steps, :])

    guess = stage[0, 0:steps, :]
    previous = jnp.concatenate([entering_from(stage[0], 0), guess[: steps - 1]], axis=0)
    row = lax.broadcasted_iota(jnp.int32, (16, BLOCK), 0) % 8

    for turn in range(NEWTON):
        if turn:
            stage[turn, 0:steps, :] = previous
            for away in range(1, n_unit):
                mate_copy(turn, away).start()

        if turn == 0:
            for load in loads:
                load.wait()
            for load in smalls[2:]:
                load.wait()
            for block in range(count):
                first = pl.multiple_of((column * count + block) * BLOCK, BLOCK)
                inputs = pl.ds(pl.multiple_of(unit * width + first, BLOCK), BLOCK)
                here = slice(block * BLOCK, (block + 1) * BLOCK)
                for gate in range(3):
                    w_diag[here, gate * BLOCK : (gate + 1) * BLOCK] = w_all[gate, inputs, pl.ds(first, BLOCK)]

        def product(panel, owner):
            first = pl.multiple_of(owner * width, width)
            panel = jnp.concatenate([panel] * (16 // steps), axis=0).astype(jnp.bfloat16)
            return [
                jnp.dot(panel, w_all[gate, pl.ds(first, width), :], preferred_element_type=jnp.float32)[:steps]
                for gate in range(3)
            ]

        rec = product(previous, unit)
        for away in range(1, n_unit):
            mate_copy(turn, away).wait_recv()
            held = mates[turn, away - 1]
            if turn:
                panel = held[:steps]
            else:
                panel = jnp.concatenate([entering_from(held, n_unit - away), held[: steps - 1]], axis=0)
            rec = [x + y for x, y in zip(rec, product(panel, lax.rem(unit + n_unit - away, n_unit)))]

        update_in = proj[0].astype(jnp.float32) + rec[0] + bias_u[...]
        update = jax.nn.sigmoid(update_in)
        fresh = jax.nn.sigmoid(-update_in)
        reset = jax.nn.sigmoid(proj[1].astype(jnp.float32) + rec[1])
        cand_rec = rec[2] + bias_c[...]
        cand = jnp.tanh(proj[2].astype(jnp.float32) + reset * cand_rec)
        coef_d = fresh * (1.0 - cand * cand) * reset
        values = (
            fresh,
            (previous - cand) * update * fresh,
            coef_d * cand_rec * (1.0 - reset),
            coef_d,
            fresh * cand + update * previous - guess,
        )
        for index, value in enumerate(values):
            for block in range(blocks):
                first = index * rows + block % count
                where = pl.ds(first, steps, stride=count) if count > 1 else pl.ds(first, steps)
                own[turn, block // count, where, :] = value[:, block * BLOCK : (block + 1) * BLOCK]
        for away in list(range(group - 1, 0, -1)) + list(range(-1, -split, -1)):
            @pl.when(coef_wanted(away))
            def _():
                coef_copy(turn, away).start()
        coefs[turn, place] = own[turn, column]

        def step(delta, five):
            high = delta.astype(jnp.bfloat16).astype(jnp.float32)
            both = jnp.concatenate([high, delta - high], axis=0)
            if count > 1:
                both = jnp.concatenate([jnp.where(row == block, both, 0.0) for block in range(count)], axis=1)
            left = both.astype(jnp.bfloat16)
            terms = jnp.dot(left, w_diag[...], preferred_element_type=jnp.float32)
            terms = terms[:8] + terms[8:]
            fresh, a, c, d, gap = five
            return (
                (gap + delta - fresh * delta) + a * terms[:, :BLOCK]
                + c * terms[:, BLOCK : 2 * BLOCK] + d * terms[:, 2 * BLOCK :]
            )

        def at_step(source, t):
            def pick(index):
                first = index * rows + t * count
                part = coefs[turn, source, first : first + count, :]
                return jnp.concatenate([part] * (8 // count), axis=0) if count > 1 else jnp.broadcast_to(part, (8, BLOCK))

            return [pick(index) for index in range(COEFS)]

        def pass_block(source, delta):
            coef_arrival(turn, source).wait_recv()
            for t in range(steps):
                delta = step(delta, at_step(source, t))
            return delta

        delta = jnp.zeros((8, BLOCK), jnp.float32)
        if n_groups > 1:
            relay_in_now = relay_in.at[turn]

            @pl.when(time < group)
            def _():
                relay_in_now[...] = jnp.zeros((8, BLOCK), jnp.float32)

            @pl.when(time >= group)
            def _():
                relay_copy(turn, 0).wait_recv()

            delta = relay_in_now[...]
        delta = lax.fori_loop(0, place - column, pass_block, delta)
        for member in range(split):
            source = place - column + member

            @pl.when(column != member)
            def _():
                coef_arrival(turn, source).wait_recv()

            found[turn, member, 0:count, :] = delta[:count]
            for t in range(steps):
                delta = step(delta, at_step(source, t))
                found[turn, member, (t + 1) * count : (t + 2) * count, :] = delta[:count]

            @pl.when(column != member)
            def _():
                move_copy(turn, member).start()

        moves[turn, column] = found[turn, column]
        if n_groups > 1:
            relay_out[turn] = delta

            @pl.when(last_row & (time < n_tm - split))
            def _():
                for target in range(group // split):
                    relay_copy(turn, target).start()

        for member in range(split):
            @pl.when(column != member)
            def _():
                move_arrival(turn, member).wait_recv()

        def moved(skip):
            parts = []
            for block in range(blocks):
                first = skip * count + block % count
                where = pl.ds(first, steps, stride=count) if count > 1 else pl.ds(first, steps)
                parts.append(moves[turn, block // count, where, :])
            return jnp.concatenate(parts, axis=1)

        guess = guess + moved(1)
        if turn < NEWTON - 1:
            previous = previous + moved(0)
    out[...] = guess

    @pl.when(time < n_tm - 1)
    def _():
        for away in range(n_unit):
            near_copy(away).wait_send()

    for turn in range(NEWTON):
        for away in range(1, n_unit):
            mate_copy(turn, away).wait_send()
        for away in range(1 - split, group):
            if away:
                @pl.when(coef_wanted(away))
                def _():
                    coef_copy(turn, away).wait_send()
        for member in range(split):
            @pl.when(column != member)
            def _():
                move_copy(turn, member).wait_send()
        if n_groups > 1:
            @pl.when(last_row & (time < n_tm - split))
            def _():
                for target in range(group // split):
                    relay_copy(turn, target).wait_send()


def shards(n_tm, n_unit, projections, recurrent, update_bias, candidate_bias, start_state, initial_guess):
    _, steps, _, width = projections.shape
    full = recurrent.shape[0]
    blocks = width // BLOCK
    group = min(GROUP, n_tm)
    split = math.gcd(blocks, group)
    count = blocks // split
    sent = 8 * pl.cdiv(COEFS * steps * count, 8)
    kept = 8 * pl.cdiv((steps + 1) * count, 8)
    vmem = pl.BlockSpec(memory_space=pltpu.VMEM)
    f32, bf16 = jnp.float32, jnp.bfloat16
    held = 8 * pl.cdiv(steps + 1, 8)
    dma = pltpu.SemaphoreType.DMA
    result = pl.pallas_call(
        functools.partial(newton_kernel, n_tm, n_unit),
        out_shape=jax.ShapeDtypeStruct((steps, width), f32),
        in_specs=[pl.BlockSpec(memory_space=pltpu.HBM)] * 6,
        out_specs=vmem,
        scratch_shapes=[
            pltpu.VMEM((3, steps, width), bf16),
            pltpu.VMEM((1, width), f32),
            pltpu.VMEM((1, width), f32),
            pltpu.VMEM((3, full, width), bf16),
            pltpu.VMEM((count * BLOCK, 3 * BLOCK), bf16),
            pltpu.VMEM((NEWTON, held, width), f32),
            pltpu.VMEM((NEWTON, n_unit - 1, held, width), f32),
            pltpu.VMEM((n_unit, held, width), f32),
            pltpu.VMEM((NEWTON, split, sent, BLOCK), f32),
            pltpu.VMEM((NEWTON, group, sent, BLOCK), f32),
            pltpu.VMEM((NEWTON, split, kept, BLOCK), f32),
            pltpu.VMEM((NEWTON, split, kept, BLOCK), f32),
            pltpu.VMEM((NEWTON, 8, BLOCK), f32),
            pltpu.VMEM((NEWTON, 8, BLOCK), f32),
            dma((5,)),
            dma((3,)),
            dma((NEWTON, n_unit - 1)),
            dma((NEWTON, n_unit - 1)),
            dma((n_unit,)),
            dma((n_unit,)),
            dma((NEWTON, group + split)),
            dma((NEWTON, group)),
            dma((NEWTON, split)),
            dma((NEWTON, split)),
            dma((NEWTON, group // split)),
            dma((NEWTON,)),
        ],
        compiler_params=pltpu.CompilerParams(
            collective_id=0, has_side_effects=True, vmem_limit_bytes=60 * 1024 * 1024
        ),
        name="newton",
    )(
        jnp.transpose(projections[0], (1, 0, 2)),
        jnp.transpose(recurrent, (1, 0, 2)),
        update_bias.reshape(1, width),
        candidate_bias.reshape(1, width),
        start_state,
        initial_guess[0],
    )
    return result[None]


def solution(mesh):
    return jax.shard_map(
        functools.partial(shards, mesh.shape["tm"], mesh.shape["unit"]),
        mesh=mesh,
        in_specs=(
            P("sweep", "tm", None, "unit"),
            P("sweep", None, "unit"),
            P(("sweep", "unit")),
            P(("sweep", "unit")),
            P("sweep", "unit"),
            P("sweep", "tm", "unit"),
        ),
        out_specs=P("sweep", "tm", "unit"),
        check_vma=False,
    )
```

```python
import functools

import jax
import jax.numpy as jnp
from jax import lax
from jax.experimental import pallas as pl
from jax.experimental.pallas import tpu as pltpu
from jax.sharding import PartitionSpec as P

BLOCK = 128
NEWTON = 2
GROUP = 8
COEFS = 5
FINE = (0, 4)
SENT = COEFS + len(FINE)
MESH = pl.DeviceIdType.MESH


def to(tm, unit):
    return {"tm": tm, "unit": unit}


def newton_kernel(
    n_tm, n_unit, proj_hbm, w_hbm, bias_u_hbm, bias_c_hbm, start_hbm, guess_hbm, out,
    proj, bias_u, bias_c, w_all, w_diag, stage, mates, nears, own, packed, coefs, moves, relay_out, relay_in,
    in_sem, w_sem, mate_send, mate_recv, near_send, near_recv, coef_send, coef_recv, relay_send, relay_recv,
):
    steps, width = guess_hbm.shape
    blocks = width // BLOCK
    rows = steps * blocks
    side = 2 if blocks % 2 == 0 else 1
    group = min(GROUP, n_tm)
    n_groups = n_tm // group
    time = lax.axis_index("tm")
    unit = lax.axis_index("unit")
    place = lax.rem(time, group)
    reach = min(n_tm - 1, group if n_groups > 1 else group - 1)

    smalls = [
        pltpu.make_async_copy(source, target, in_sem.at[index])
        for index, (source, target) in enumerate((
            (guess_hbm, stage.at[0, pl.ds(0, steps)]),
            (start_hbm, stage.at[0, pl.ds(steps, 1)]),
            (proj_hbm, proj),
            (bias_u_hbm, bias_u),
            (bias_c_hbm, bias_c),
        ))
    ]
    for load in smalls:
        load.start()
    loads = [
        pltpu.make_async_copy(w_hbm.at[gate], w_all.at[gate], w_sem.at[gate]) for gate in range(3)
    ]
    for load in loads:
        load.start()

    barrier = pltpu.get_barrier_semaphore()
    greeted = jnp.int32(n_unit - 1)
    for away in range(1, n_unit):
        pl.semaphore_signal(
            barrier, inc=1, device_id=to(time, lax.rem(unit + away, n_unit)), device_id_type=MESH
        )
    for away in range(1, reach + 1):
        turns = range(n_unit if away == 1 else 1)
        for there, valid in ((time + away, time + away < n_tm), (time - away, time >= away)):
            greeted = greeted + jnp.where(valid, len(turns), 0)

            @pl.when(valid)
            def _():
                for turn in turns:
                    pl.semaphore_signal(
                        barrier, inc=1, device_id=to(there, lax.rem(unit + turn, n_unit)), device_id_type=MESH
                    )

    for load in smalls[:2]:
        load.wait()
    pl.semaphore_wait(barrier, greeted)

    def mate_copy(turn, away):
        return pltpu.make_async_remote_copy(
            src_ref=stage.at[turn], dst_ref=mates.at[turn, away - 1],
            send_sem=mate_send.at[turn, away - 1], recv_sem=mate_recv.at[turn, away - 1],
            device_id=to(time, lax.rem(unit + away, n_unit)), device_id_type=MESH,
        )

    def near_copy(away):
        return pltpu.make_async_remote_copy(
            src_ref=stage.at[0], dst_ref=nears.at[away],
            send_sem=near_send.at[away], recv_sem=near_recv.at[away],
            device_id=to(lax.rem(time + 1, n_tm), lax.rem(unit + away, n_unit)), device_id_type=MESH,
        )

    def coef_copy(turn, away):
        return pltpu.make_async_remote_copy(
            src_ref=packed.at[turn], dst_ref=coefs.at[turn, away - 1],
            send_sem=coef_send.at[turn, away - 1], recv_sem=coef_recv.at[turn, away - 1],
            device_id=to(lax.rem(time + away, n_tm), unit), device_id_type=MESH,
        )

    def relay_copy(turn, target):
        return pltpu.make_async_remote_copy(
            src_ref=relay_out.at[turn], dst_ref=relay_in.at[turn],
            send_sem=relay_send.at[turn, target], recv_sem=relay_recv.at[turn],
            device_id=to(lax.rem(time + 1 + target, n_tm), unit), device_id_type=MESH,
        )

    for away in range(1, n_unit):
        mate_copy(0, away).start()

    @pl.when(time < n_tm - 1)
    def _():
        for away in range(n_unit):
            near_copy(away).start()

    @pl.when(time > 0)
    def _():
        for away in range(n_unit):
            near_copy(away).wait_recv()

    def entering_from(held, away):
        return jnp.where(time == 0, held[steps : steps + 1, :], nears[(n_unit - away) % n_unit, steps - 1 : steps, :])

    guess = stage[0, 0:steps, :]
    previous = jnp.concatenate([entering_from(stage[0], 0), guess[: steps - 1]], axis=0)
    row = lax.broadcasted_iota(jnp.int32, (8, BLOCK), 0)

    def gate_column(pair, gate):
        pairs = blocks // side
        return (2 * pair + gate if gate < 2 else 2 * pairs + pair) * BLOCK


    for turn in range(NEWTON):
        if turn:
            stage[turn, 0:steps, :] = previous
            for away in range(1, n_unit):
                mate_copy(turn, away).start()

        if turn == 0:
            for load in loads:
                load.wait()
            for load in smalls[2:]:
                load.wait()
            for block in range(blocks):
                first = pl.multiple_of(unit * width + block * BLOCK, BLOCK)
                here = slice(block * BLOCK, (block + 1) * BLOCK)
                depth = block % side * BLOCK
                for gate in range(3):
                    column = gate_column(block // side, gate)
                    w_diag[depth : depth + BLOCK, column : column + BLOCK] = w_all[gate, pl.ds(first, BLOCK), here]

        def product(panel, owner):
            first = pl.multiple_of(owner * width, width)
            panel = jnp.concatenate([panel] * (16 // steps), axis=0).astype(jnp.bfloat16)
            return [
                jnp.dot(panel, w_all[gate, pl.ds(first, width), :], preferred_element_type=jnp.float32)[:steps]
                for gate in range(3)
            ]

        def step(delta, five):
            left = jnp.concatenate(
                [jnp.where((row % side == depth) & (row < blocks), delta, 0.0) for depth in range(side)], axis=1
            ).astype(jnp.bfloat16)
            terms = jnp.dot(left, w_diag[...], preferred_element_type=jnp.float32)

            def of_gate(gate):
                value = None
                for pair in range(blocks // side):
                    column = gate_column(pair, gate)
                    part = terms[:, column : column + BLOCK]
                    value = part if value is None else jnp.where(row // side == pair, part, value)
                return value

            fresh, a, c, d, gap = five
            return (
                (gap + delta - fresh * delta) + a * of_gate(0) + c * of_gate(1) + d * of_gate(2)
            )

        def at_step(table, t):
            def pick(value):
                part = value[t * blocks : (t + 1) * blocks]
                return jnp.concatenate([part] * (8 // blocks), axis=0)

            return [pick(table[index]) for index in range(COEFS)]

        def pass_block(source, delta):
            away = place - source
            slot = away - 1
            pltpu.make_async_remote_copy(
                src_ref=packed.at[turn], dst_ref=coefs.at[turn, slot],
                send_sem=coef_send.at[turn, slot], recv_sem=coef_recv.at[turn, slot],
                device_id=to(lax.rem(time + 1, n_tm), unit), device_id_type=MESH,
            ).wait_recv()
            table = [coefs[turn, slot, index].astype(jnp.float32) for index in range(SENT)]
            for low, index in enumerate(FINE):
                table[index] = table[index] + table[COEFS + low]
            for t in range(steps):
                delta = step(delta, at_step(table, t))
            return delta

        rec = product(previous, unit)
        early = jnp.int32(0)
        if turn == 0 or n_groups > 1:
            delta = jnp.zeros((8, BLOCK), jnp.float32)
        else:
            early = (2 * place) // group
            delta = lax.fori_loop(0, early, pass_block, jnp.zeros((8, BLOCK), jnp.float32))
        for away in range(1, n_unit):
            mate_copy(turn, away).wait_recv()
            held = mates[turn, away - 1]
            if turn:
                panel = held[:steps]
            else:
                panel = jnp.concatenate([entering_from(held, n_unit - away), held[: steps - 1]], axis=0)
            rec = [x + y for x, y in zip(rec, product(panel, lax.rem(unit + n_unit - away, n_unit)))]

        update_in = proj[0].astype(jnp.float32) + rec[0] + bias_u[...]
        update = jax.nn.sigmoid(update_in)
        fresh = jax.nn.sigmoid(-update_in)
        reset = jax.nn.sigmoid(proj[1].astype(jnp.float32) + rec[1])
        cand_rec = rec[2] + bias_c[...]
        cand = jnp.tanh(proj[2].astype(jnp.float32) + reset * cand_rec)
        coef_d = fresh * (1.0 - cand * cand) * reset
        values = (
            fresh,
            (previous - cand) * update * fresh,
            coef_d * cand_rec * (1.0 - reset),
            coef_d,
            fresh * cand + update * previous - guess,
        )
        for index, value in enumerate(values):
            for block in range(blocks):
                own[index, pl.ds(block, steps, stride=blocks), :] = value[:, block * BLOCK : (block + 1) * BLOCK]
        packed[turn, 0:COEFS] = own[...].astype(jnp.bfloat16)
        for slot, index in enumerate(FINE):
            full = own[index]
            packed[turn, COEFS + slot] = (full - full.astype(jnp.bfloat16).astype(jnp.float32)).astype(jnp.bfloat16)

        for away in range(group - 1, 0, -1):
            @pl.when(place + away < group)
            def _():
                coef_copy(turn, away).start()

        if n_groups > 1:
            relay_in_now = relay_in.at[turn]

            @pl.when(time < group)
            def _():
                relay_in_now[...] = jnp.zeros((8, BLOCK), jnp.float32)

            @pl.when(time >= group)
            def _():
                relay_copy(turn, 0).wait_recv()

            delta = relay_in_now[...]
        delta = lax.fori_loop(early, place, pass_block, delta)
        moves[0:blocks, :] = delta[:blocks]
        table = own[...]
        for t in range(steps):
            delta = step(delta, at_step(table, t))
            moves[(t + 1) * blocks : (t + 2) * blocks, :] = delta[:blocks]
        if n_groups > 1:
            relay_out[turn] = delta

            @pl.when((place == group - 1) & (time < n_tm - 1))
            def _():
                for target in range(group):
                    relay_copy(turn, target).start()

        def moved(skip):
            return jnp.concatenate(
                [moves[pl.ds(skip * blocks + block, steps, stride=blocks), :] for block in range(blocks)], axis=1
            )

        guess = guess + moved(1)
        if turn < NEWTON - 1:
            previous = previous + moved(0)
    out[...] = guess

    @pl.when(time < n_tm - 1)
    def _():
        for away in range(n_unit):
            near_copy(away).wait_send()

    for turn in range(NEWTON):
        for away in range(1, n_unit):
            mate_copy(turn, away).wait_send()
        for away in range(1, group):
            @pl.when(place + away < group)
            def _():
                coef_copy(turn, away).wait_send()
        if n_groups > 1:
            @pl.when((place == group - 1) & (time < n_tm - 1))
            def _():
                for target in range(group):
                    relay_copy(turn, target).wait_send()


def shards(n_tm, n_unit, projections, recurrent, update_bias, candidate_bias, start_state, initial_guess):
    _, steps, _, width = projections.shape
    full = recurrent.shape[0]
    rows = steps * (width // BLOCK)
    group = min(GROUP, n_tm)
    side = 2 if width // BLOCK % 2 == 0 else 1
    vmem = pl.BlockSpec(memory_space=pltpu.VMEM)
    f32, bf16 = jnp.float32, jnp.bfloat16
    held = 8 * pl.cdiv(steps + 1, 8)
    dma = pltpu.SemaphoreType.DMA
    result = pl.pallas_call(
        functools.partial(newton_kernel, n_tm, n_unit),
        out_shape=jax.ShapeDtypeStruct((steps, width), f32),
        in_specs=[pl.BlockSpec(memory_space=pltpu.HBM)] * 6,
        out_specs=vmem,
        scratch_shapes=[
            pltpu.VMEM((3, steps, width), bf16),
            pltpu.VMEM((1, width), f32),
            pltpu.VMEM((1, width), f32),
            pltpu.VMEM((3, full, width), bf16),
            pltpu.VMEM((side * BLOCK, 3 * (width // side)), bf16),
            pltpu.VMEM((NEWTON, held, width), f32),
            pltpu.VMEM((NEWTON, n_unit - 1, held, width), f32),
            pltpu.VMEM((n_unit, held, width), f32),
            pltpu.VMEM((COEFS, rows, BLOCK), f32),
            pltpu.VMEM((NEWTON, SENT, rows, BLOCK), bf16),
            pltpu.VMEM((NEWTON, group - 1, SENT, rows, BLOCK), bf16),
            pltpu.VMEM((rows + 8, BLOCK), f32),
            pltpu.VMEM((NEWTON, 8, BLOCK), f32),
            pltpu.VMEM((NEWTON, 8, BLOCK), f32),
            dma((5,)),
            dma((3,)),
            dma((NEWTON, n_unit - 1)),
            dma((NEWTON, n_unit - 1)),
            dma((n_unit,)),
            dma((n_unit,)),
            dma((NEWTON, group - 1)),
            dma((NEWTON, group - 1)),
            dma((NEWTON, group)),
            dma((NEWTON,)),
        ],
        compiler_params=pltpu.CompilerParams(
            collective_id=0, has_side_effects=True, vmem_limit_bytes=60 * 1024 * 1024
        ),
        name="newton",
    )(
        jnp.transpose(projections[0], (1, 0, 2)),
        jnp.transpose(recurrent, (1, 0, 2)),
        update_bias.reshape(1, width),
        candidate_bias.reshape(1, width),
        start_state,
        initial_guess[0],
    )
    return result[None]


def solution(mesh):
    return jax.shard_map(
        functools.partial(shards, mesh.shape["tm"], mesh.shape["unit"]),
        mesh=mesh,
        in_specs=(
            P("sweep", "tm", None, "unit"),
            P("sweep", None, "unit"),
            P(("sweep", "unit")),
            P(("sweep", "unit")),
            P("sweep", "unit"),
            P("sweep", "tm", "unit"),
        ),
        out_specs=P("sweep", "tm", "unit"),
        check_vma=False,
    )
```

```python
import functools

import jax
import jax.numpy as jnp
from jax import lax
from jax.experimental import pallas as pl
from jax.experimental.pallas import tpu as pltpu
from jax.sharding import PartitionSpec as P

BLOCK = 128
NEWTON = 2
GROUP = 8
COEFS = 5
FINE = (0, 4)
SENT = COEFS + len(FINE)
MESH = pl.DeviceIdType.MESH


def to(tm, unit):
    return {"tm": tm, "unit": unit}


def newton_kernel(
    n_tm, n_unit, proj_hbm, w_hbm, bias_u_hbm, bias_c_hbm, start_hbm, guess_hbm, out,
    proj, bias_u, bias_c, w_all, w_diag, stage, mates, nears, own, packed, coefs, moves, relay_out, relay_in,
    in_sem, w_sem, mate_send, mate_recv, near_send, near_recv, coef_send, coef_recv, pass_send, relay_send, relay_recv,
):
    steps, width = guess_hbm.shape
    blocks = width // BLOCK
    rows = steps * blocks
    side = 2 if blocks % 2 == 0 else 1
    group = min(GROUP, n_tm)
    n_groups = n_tm // group
    time = lax.axis_index("tm")
    unit = lax.axis_index("unit")
    place = lax.rem(time, group)
    side_of = lax.rem(place, 2)
    pair_row = lax.div(place, 2)
    straight = [away for away in range(group - 1, 0, -1) if away == 1 or away % 2 == 0]
    reach = min(n_tm - 1, group if n_groups > 1 else group - 1)

    smalls = [
        pltpu.make_async_copy(source, target, in_sem.at[index])
        for index, (source, target) in enumerate((
            (guess_hbm, stage.at[0, pl.ds(0, steps)]),
            (start_hbm, stage.at[0, pl.ds(steps, 1)]),
            (proj_hbm, proj),
            (bias_u_hbm, bias_u),
            (bias_c_hbm, bias_c),
        ))
    ]
    for load in smalls:
        load.start()
    loads = [
        pltpu.make_async_copy(w_hbm.at[gate], w_all.at[gate], w_sem.at[gate]) for gate in range(3)
    ]
    for load in loads:
        load.start()

    barrier = pltpu.get_barrier_semaphore()
    greeted = jnp.int32(n_unit - 1)
    for away in range(1, n_unit):
        pl.semaphore_signal(
            barrier, inc=1, device_id=to(time, lax.rem(unit + away, n_unit)), device_id_type=MESH
        )
    for away in range(1, reach + 1):
        turns = range(n_unit if away == 1 else 1)
        for there, valid in ((time + away, time + away < n_tm), (time - away, time >= away)):
            greeted = greeted + jnp.where(valid, len(turns), 0)

            @pl.when(valid)
            def _():
                for turn in turns:
                    pl.semaphore_signal(
                        barrier, inc=1, device_id=to(there, lax.rem(unit + turn, n_unit)), device_id_type=MESH
                    )

    for load in smalls[:2]:
        load.wait()
    pl.semaphore_wait(barrier, greeted)

    def mate_copy(turn, away):
        return pltpu.make_async_remote_copy(
            src_ref=stage.at[turn], dst_ref=mates.at[turn, away - 1],
            send_sem=mate_send.at[turn, away - 1], recv_sem=mate_recv.at[turn, away - 1],
            device_id=to(time, lax.rem(unit + away, n_unit)), device_id_type=MESH,
        )

    def near_copy(away):
        return pltpu.make_async_remote_copy(
            src_ref=stage.at[0], dst_ref=nears.at[away],
            send_sem=near_send.at[away], recv_sem=near_recv.at[away],
            device_id=to(lax.rem(time + 1, n_tm), lax.rem(unit + away, n_unit)), device_id_type=MESH,
        )

    def coef_copy(turn, away):
        return pltpu.make_async_remote_copy(
            src_ref=packed.at[turn], dst_ref=coefs.at[turn, away - 1],
            send_sem=coef_send.at[turn, away - 1], recv_sem=coef_recv.at[turn, away - 1],
            device_id=to(lax.rem(time + away, n_tm), unit), device_id_type=MESH,
        )

    def pass_on(turn, distance):
        return pltpu.make_async_remote_copy(
            src_ref=coefs.at[turn, distance - 1], dst_ref=coefs.at[turn, distance - 2 * side_of],
            send_sem=pass_send.at[turn, lax.div(distance, 2) - 1], recv_sem=coef_recv.at[turn, distance - 2 * side_of],
            device_id=to(time + 1 - 2 * side_of, unit), device_id_type=MESH,
        )

    def relay_copy(turn, target):
        return pltpu.make_async_remote_copy(
            src_ref=relay_out.at[turn], dst_ref=relay_in.at[turn],
            send_sem=relay_send.at[turn, target], recv_sem=relay_recv.at[turn],
            device_id=to(lax.rem(time + 1 + target, n_tm), unit), device_id_type=MESH,
        )

    for away in range(1, n_unit):
        mate_copy(0, away).start()

    @pl.when(time < n_tm - 1)
    def _():
        for away in range(n_unit):
            near_copy(away).start()

    @pl.when(time > 0)
    def _():
        for away in range(n_unit):
            near_copy(away).wait_recv()

    def entering_from(held, away):
        return jnp.where(time == 0, held[steps : steps + 1, :], nears[(n_unit - away) % n_unit, steps - 1 : steps, :])

    guess = stage[0, 0:steps, :]
    previous = jnp.concatenate([entering_from(stage[0], 0), guess[: steps - 1]], axis=0)
    row = lax.broadcasted_iota(jnp.int32, (8, BLOCK), 0)

    def gate_column(pair, gate):
        pairs = blocks // side
        return (2 * pair + gate if gate < 2 else 2 * pairs + pair) * BLOCK


    for turn in range(NEWTON):
        if turn:
            stage[turn, 0:steps, :] = previous
            for away in range(1, n_unit):
                mate_copy(turn, away).start()

        if turn == 0:
            for load in loads:
                load.wait()
            for load in smalls[2:]:
                load.wait()
            for block in range(blocks):
                first = pl.multiple_of(unit * width + block * BLOCK, BLOCK)
                here = slice(block * BLOCK, (block + 1) * BLOCK)
                depth = block % side * BLOCK
                for gate in range(3):
                    column = gate_column(block // side, gate)
                    w_diag[depth : depth + BLOCK, column : column + BLOCK] = w_all[gate, pl.ds(first, BLOCK), here]

        def product(panel, owner):
            first = pl.multiple_of(owner * width, width)
            panel = jnp.concatenate([panel] * (16 // steps), axis=0).astype(jnp.bfloat16)
            return [
                jnp.dot(panel, w_all[gate, pl.ds(first, width), :], preferred_element_type=jnp.float32)[:steps]
                for gate in range(3)
            ]

        def step(delta, five):
            left = jnp.concatenate(
                [jnp.where((row % side == depth) & (row < blocks), delta, 0.0) for depth in range(side)], axis=1
            ).astype(jnp.bfloat16)
            terms = jnp.dot(left, w_diag[...], preferred_element_type=jnp.float32)

            def of_gate(gate):
                value = None
                for pair in range(blocks // side):
                    column = gate_column(pair, gate)
                    part = terms[:, column : column + BLOCK]
                    value = part if value is None else jnp.where(row // side == pair, part, value)
                return value

            fresh, a, c, d, gap = five
            return (
                (gap + delta - fresh * delta) + a * of_gate(0) + c * of_gate(1) + d * of_gate(2)
            )

        def at_step(table, t):
            def pick(value):
                part = value[t * blocks : (t + 1) * blocks]
                return jnp.concatenate([part] * (8 // blocks), axis=0)

            return [pick(table[index]) for index in range(COEFS)]

        def arrival(slot):
            pltpu.make_async_remote_copy(
                src_ref=packed.at[turn], dst_ref=coefs.at[turn, slot],
                send_sem=coef_send.at[turn, slot], recv_sem=coef_recv.at[turn, slot],
                device_id=to(lax.rem(time + 1, n_tm), unit), device_id_type=MESH,
            ).wait_recv()

        def take(pair):
            distance = 2 * (pair_row - pair)
            arrival(distance - 1)

            @pl.when((side_of == 0) | (distance >= 4))
            def _():
                pass_on(turn, distance).start()

        def pass_block(slot, delta):
            table = [coefs[turn, slot, index].astype(jnp.float32) for index in range(SENT)]
            for low, index in enumerate(FINE):
                table[index] = table[index] + table[COEFS + low]
            for t in range(steps):
                delta = step(delta, at_step(table, t))
            return delta

        def pass_pair(pair, delta):
            @pl.when(pair + 1 < pair_row)
            def _():
                take(pair + 1)

            slot = place - 2 * pair - 1

            @pl.when(side_of == 1)
            def _():
                arrival(slot)

            delta = pass_block(slot, delta)

            @pl.when(side_of == 0)
            def _():
                arrival(slot - 1)

            return pass_block(slot - 1, delta)

        def pass_last(_, delta):
            arrival(0)
            return pass_block(0, delta)

        rec = product(previous, unit)
        for away in range(1, n_unit):
            mate_copy(turn, away).wait_recv()
            held = mates[turn, away - 1]
            if turn:
                panel = held[:steps]
            else:
                panel = jnp.concatenate([entering_from(held, n_unit - away), held[: steps - 1]], axis=0)
            rec = [x + y for x, y in zip(rec, product(panel, lax.rem(unit + n_unit - away, n_unit)))]

        update_in = proj[0].astype(jnp.float32) + rec[0] + bias_u[...]
        update = jax.nn.sigmoid(update_in)
        fresh = jax.nn.sigmoid(-update_in)
        reset = jax.nn.sigmoid(proj[1].astype(jnp.float32) + rec[1])
        cand_rec = rec[2] + bias_c[...]
        cand = jnp.tanh(proj[2].astype(jnp.float32) + reset * cand_rec)
        coef_d = fresh * (1.0 - cand * cand) * reset
        values = (
            fresh,
            (previous - cand) * update * fresh,
            coef_d * cand_rec * (1.0 - reset),
            coef_d,
            fresh * cand + update * previous - guess,
        )
        for index, value in enumerate(values):
            for block in range(blocks):
                own[index, pl.ds(block, steps, stride=blocks), :] = value[:, block * BLOCK : (block + 1) * BLOCK]
        packed[turn, 0:COEFS] = own[...].astype(jnp.bfloat16)
        for slot, index in enumerate(FINE):
            full = own[index]
            packed[turn, COEFS + slot] = (full - full.astype(jnp.bfloat16).astype(jnp.float32)).astype(jnp.bfloat16)

        for away in straight:
            @pl.when(place + away < group)
            def _():
                coef_copy(turn, away).start()

        @pl.when(pair_row > 0)
        def _():
            take(0)

        delta = jnp.zeros((8, BLOCK), jnp.float32)
        if n_groups > 1:
            relay_in_now = relay_in.at[turn]

            @pl.when(time < group)
            def _():
                relay_in_now[...] = jnp.zeros((8, BLOCK), jnp.float32)

            @pl.when(time >= group)
            def _():
                relay_copy(turn, 0).wait_recv()

            delta = relay_in_now[...]
        delta = lax.fori_loop(0, pair_row, pass_pair, delta)
        delta = lax.fori_loop(0, side_of, pass_last, delta)
        moves[0:blocks, :] = delta[:blocks]
        table = own[...]
        for t in range(steps):
            delta = step(delta, at_step(table, t))
            moves[(t + 1) * blocks : (t + 2) * blocks, :] = delta[:blocks]
        if n_groups > 1:
            relay_out[turn] = delta

            @pl.when((place == group - 1) & (time < n_tm - 1))
            def _():
                for target in range(group):
                    relay_copy(turn, target).start()

        def moved(skip):
            return jnp.concatenate(
                [moves[pl.ds(skip * blocks + block, steps, stride=blocks), :] for block in range(blocks)], axis=1
            )

        guess = guess + moved(1)
        if turn < NEWTON - 1:
            previous = previous + moved(0)
    out[...] = guess

    @pl.when(time < n_tm - 1)
    def _():
        for away in range(n_unit):
            near_copy(away).wait_send()

    for turn in range(NEWTON):
        for away in range(1, n_unit):
            mate_copy(turn, away).wait_send()
        for away in straight:
            @pl.when(place + away < group)
            def _():
                coef_copy(turn, away).wait_send()
        for distance in range(2, group, 2):
            @pl.when((place >= distance) & ((side_of == 0) | (distance >= 4)))
            def _():
                pass_on(turn, distance).wait_send()
        if n_groups > 1:
            @pl.when((place == group - 1) & (time < n_tm - 1))
            def _():
                for target in range(group):
                    relay_copy(turn, target).wait_send()


def shards(n_tm, n_unit, projections, recurrent, update_bias, candidate_bias, start_state, initial_guess):
    _, steps, _, width = projections.shape
    full = recurrent.shape[0]
    rows = steps * (width // BLOCK)
    group = min(GROUP, n_tm)
    side = 2 if width // BLOCK % 2 == 0 else 1
    vmem = pl.BlockSpec(memory_space=pltpu.VMEM)
    f32, bf16 = jnp.float32, jnp.bfloat16
    held = 8 * pl.cdiv(steps + 1, 8)
    dma = pltpu.SemaphoreType.DMA
    result = pl.pallas_call(
        functools.partial(newton_kernel, n_tm, n_unit),
        out_shape=jax.ShapeDtypeStruct((steps, width), f32),
        in_specs=[pl.BlockSpec(memory_space=pltpu.HBM)] * 6,
        out_specs=vmem,
        scratch_shapes=[
            pltpu.VMEM((3, steps, width), bf16),
            pltpu.VMEM((1, width), f32),
            pltpu.VMEM((1, width), f32),
            pltpu.VMEM((3, full, width), bf16),
            pltpu.VMEM((side * BLOCK, 3 * (width // side)), bf16),
            pltpu.VMEM((NEWTON, held, width), f32),
            pltpu.VMEM((NEWTON, n_unit - 1, held, width), f32),
            pltpu.VMEM((n_unit, held, width), f32),
            pltpu.VMEM((COEFS, rows, BLOCK), f32),
            pltpu.VMEM((NEWTON, SENT, rows, BLOCK), bf16),
            pltpu.VMEM((NEWTON, group - 1, SENT, rows, BLOCK), bf16),
            pltpu.VMEM((rows + 8, BLOCK), f32),
            pltpu.VMEM((NEWTON, 8, BLOCK), f32),
            pltpu.VMEM((NEWTON, 8, BLOCK), f32),
            dma((5,)),
            dma((3,)),
            dma((NEWTON, n_unit - 1)),
            dma((NEWTON, n_unit - 1)),
            dma((n_unit,)),
            dma((n_unit,)),
            dma((NEWTON, group - 1)),
            dma((NEWTON, group - 1)),
            dma((NEWTON, group // 2)),
            dma((NEWTON, group)),
            dma((NEWTON,)),
        ],
        compiler_params=pltpu.CompilerParams(
            collective_id=0, has_side_effects=True, vmem_limit_bytes=60 * 1024 * 1024
        ),
        name="newton",
    )(
        jnp.transpose(projections[0], (1, 0, 2)),
        jnp.transpose(recurrent, (1, 0, 2)),
        update_bias.reshape(1, width),
        candidate_bias.reshape(1, width),
        start_state,
        initial_guess[0],
    )
    return result[None]


def solution(mesh):
    return jax.shard_map(
        functools.partial(shards, mesh.shape["tm"], mesh.shape["unit"]),
        mesh=mesh,
        in_specs=(
            P("sweep", "tm", None, "unit"),
            P("sweep", None, "unit"),
            P(("sweep", "unit")),
            P(("sweep", "unit")),
            P("sweep", "unit"),
            P("sweep", "tm", "unit"),
        ),
        out_specs=P("sweep", "tm", "unit"),
        check_vma=False,
    )
```

```python
import functools

import jax
import jax.numpy as jnp
from jax import lax
from jax.experimental import pallas as pl
from jax.experimental.pallas import tpu as pltpu
from jax.sharding import PartitionSpec as P

BLOCK = 128
NEWTON = 2
GROUP = 2
COEFS = 5
FINE = (0, 4)
SENT = COEFS + len(FINE)
MESH = pl.DeviceIdType.MESH


def to(tm, unit):
    return {"tm": tm, "unit": unit}


def newton_kernel(
    n_tm, n_unit, proj_hbm, w_hbm, bias_u_hbm, bias_c_hbm, start_hbm, guess_hbm, out,
    proj, bias_u, bias_c, w_all, w_diag, stage, mates, nears, own, packed, coefs, moves, relay_out, relay_in,
    in_sem, w_sem, mate_send, mate_recv, near_send, near_recv, coef_send, coef_recv, relay_send, relay_recv,
):
    steps, width = guess_hbm.shape
    blocks = width // BLOCK
    rows = steps * blocks
    side = 2 if blocks % 2 == 0 else 1
    group = min(GROUP, n_tm)
    n_groups = n_tm // group
    time = lax.axis_index("tm")
    unit = lax.axis_index("unit")
    place = lax.rem(time, group)
    reach = min(n_tm - 1, group if n_groups > 1 else group - 1)

    smalls = [
        pltpu.make_async_copy(source, target, in_sem.at[index])
        for index, (source, target) in enumerate((
            (guess_hbm, stage.at[0, pl.ds(0, steps)]),
            (start_hbm, stage.at[0, pl.ds(steps, 1)]),
            (proj_hbm, proj),
            (bias_u_hbm, bias_u),
            (bias_c_hbm, bias_c),
        ))
    ]
    for load in smalls:
        load.start()
    loads = [
        pltpu.make_async_copy(w_hbm.at[gate], w_all.at[gate], w_sem.at[gate]) for gate in range(3)
    ]
    for load in loads:
        load.start()

    barrier = pltpu.get_barrier_semaphore()
    greeted = jnp.int32(n_unit - 1)
    for away in range(1, n_unit):
        pl.semaphore_signal(
            barrier, inc=1, device_id=to(time, lax.rem(unit + away, n_unit)), device_id_type=MESH
        )
    for away in range(1, reach + 1):
        turns = range(n_unit if away == 1 else 1)
        for there, valid in ((time + away, time + away < n_tm), (time - away, time >= away)):
            greeted = greeted + jnp.where(valid, len(turns), 0)

            @pl.when(valid)
            def _():
                for turn in turns:
                    pl.semaphore_signal(
                        barrier, inc=1, device_id=to(there, lax.rem(unit + turn, n_unit)), device_id_type=MESH
                    )

    for load in smalls[:2]:
        load.wait()
    pl.semaphore_wait(barrier, greeted)

    def mate_copy(turn, away):
        return pltpu.make_async_remote_copy(
            src_ref=stage.at[turn], dst_ref=mates.at[turn, away - 1],
            send_sem=mate_send.at[turn, away - 1], recv_sem=mate_recv.at[turn, away - 1],
            device_id=to(time, lax.rem(unit + away, n_unit)), device_id_type=MESH,
        )

    def near_copy(away):
        return pltpu.make_async_remote_copy(
            src_ref=stage.at[0], dst_ref=nears.at[away],
            send_sem=near_send.at[away], recv_sem=near_recv.at[away],
            device_id=to(lax.rem(time + 1, n_tm), lax.rem(unit + away, n_unit)), device_id_type=MESH,
        )

    def coef_copy(turn, away):
        return pltpu.make_async_remote_copy(
            src_ref=packed.at[turn], dst_ref=coefs.at[turn, away - 1],
            send_sem=coef_send.at[turn, away - 1], recv_sem=coef_recv.at[turn, away - 1],
            device_id=to(lax.rem(time + away, n_tm), unit), device_id_type=MESH,
        )

    def relay_copy(turn, target):
        return pltpu.make_async_remote_copy(
            src_ref=relay_out.at[turn], dst_ref=relay_in.at[turn],
            send_sem=relay_send.at[turn, target], recv_sem=relay_recv.at[turn],
            device_id=to(lax.rem(time + 1 + target, n_tm), unit), device_id_type=MESH,
        )

    for away in range(1, n_unit):
        mate_copy(0, away).start()

    @pl.when(time < n_tm - 1)
    def _():
        for away in range(n_unit):
            near_copy(away).start()

    @pl.when(time > 0)
    def _():
        for away in range(n_unit):
            near_copy(away).wait_recv()

    def entering_from(held, away):
        return jnp.where(time == 0, held[steps : steps + 1, :], nears[(n_unit - away) % n_unit, steps - 1 : steps, :])

    guess = stage[0, 0:steps, :]
    previous = jnp.concatenate([entering_from(stage[0], 0), guess[: steps - 1]], axis=0)
    row = lax.broadcasted_iota(jnp.int32, (8, BLOCK), 0)

    def gate_column(pair, gate):
        pairs = blocks // side
        return (2 * pair + gate if gate < 2 else 2 * pairs + pair) * BLOCK


    for turn in range(NEWTON):
        if turn:
            stage[turn, 0:steps, :] = previous
            for away in range(1, n_unit):
                mate_copy(turn, away).start()

        if turn == 0:
            for load in loads:
                load.wait()
            for load in smalls[2:]:
                load.wait()
            for block in range(blocks):
                first = pl.multiple_of(unit * width + block * BLOCK, BLOCK)
                here = slice(block * BLOCK, (block + 1) * BLOCK)
                depth = block % side * BLOCK
                for gate in range(3):
                    column = gate_column(block // side, gate)
                    w_diag[depth : depth + BLOCK, column : column + BLOCK] = w_all[gate, pl.ds(first, BLOCK), here]

        def product(panel, owner):
            first = pl.multiple_of(owner * width, width)
            panel = jnp.concatenate([panel] * (16 // steps), axis=0).astype(jnp.bfloat16)
            return [
                jnp.dot(panel, w_all[gate, pl.ds(first, width), :], preferred_element_type=jnp.float32)[:steps]
                for gate in range(3)
            ]

        def step(delta, five):
            left = jnp.concatenate(
                [jnp.where((row % side == depth) & (row < blocks), delta, 0.0) for depth in range(side)], axis=1
            ).astype(jnp.bfloat16)
            terms = jnp.dot(left, w_diag[...], preferred_element_type=jnp.float32)

            def of_gate(gate):
                value = None
                for pair in range(blocks // side):
                    column = gate_column(pair, gate)
                    part = terms[:, column : column + BLOCK]
                    value = part if value is None else jnp.where(row // side == pair, part, value)
                return value

            fresh, a, c, d, gap = five
            return (
                (gap + delta - fresh * delta) + a * of_gate(0) + c * of_gate(1) + d * of_gate(2)
            )

        def at_step(table, t):
            def pick(value):
                part = value[t * blocks : (t + 1) * blocks]
                return jnp.concatenate([part] * (8 // blocks), axis=0)

            return [pick(table[index]) for index in range(COEFS)]

        def pass_block(source, delta):
            away = place - source
            slot = away - 1
            pltpu.make_async_remote_copy(
                src_ref=packed.at[turn], dst_ref=coefs.at[turn, slot],
                send_sem=coef_send.at[turn, slot], recv_sem=coef_recv.at[turn, slot],
                device_id=to(lax.rem(time + 1, n_tm), unit), device_id_type=MESH,
            ).wait_recv()
            table = [coefs[turn, slot, index].astype(jnp.float32) for index in range(SENT)]
            for low, index in enumerate(FINE):
                table[index] = table[index] + table[COEFS + low]
            for t in range(steps):
                delta = step(delta, at_step(table, t))
            return delta

        rec = product(previous, unit)
        early = jnp.int32(0)
        if turn == 0 or n_groups > 1:
            delta = jnp.zeros((8, BLOCK), jnp.float32)
        else:
            early = (2 * place) // group
            delta = lax.fori_loop(0, early, pass_block, jnp.zeros((8, BLOCK), jnp.float32))
        for away in range(1, n_unit):
            mate_copy(turn, away).wait_recv()
            held = mates[turn, away - 1]
            if turn:
                panel = held[:steps]
            else:
                panel = jnp.concatenate([entering_from(held, n_unit - away), held[: steps - 1]], axis=0)
            rec = [x + y for x, y in zip(rec, product(panel, lax.rem(unit + n_unit - away, n_unit)))]

        update_in = proj[0].astype(jnp.float32) + rec[0] + bias_u[...]
        update = jax.nn.sigmoid(update_in)
        fresh = jax.nn.sigmoid(-update_in)
        reset = jax.nn.sigmoid(proj[1].astype(jnp.float32) + rec[1])
        cand_rec = rec[2] + bias_c[...]
        cand = jnp.tanh(proj[2].astype(jnp.float32) + reset * cand_rec)
        coef_d = fresh * (1.0 - cand * cand) * reset
        values = (
            fresh,
            (previous - cand) * update * fresh,
            coef_d * cand_rec * (1.0 - reset),
            coef_d,
            fresh * cand + update * previous - guess,
        )
        for index, value in enumerate(values):
            for block in range(blocks):
                own[index, pl.ds(block, steps, stride=blocks), :] = value[:, block * BLOCK : (block + 1) * BLOCK]
        packed[turn, 0:COEFS] = own[...].astype(jnp.bfloat16)
        for slot, index in enumerate(FINE):
            full = own[index]
            packed[turn, COEFS + slot] = (full - full.astype(jnp.bfloat16).astype(jnp.float32)).astype(jnp.bfloat16)

        for away in range(group - 1, 0, -1):
            @pl.when(place + away < group)
            def _():
                coef_copy(turn, away).start()

        if n_groups > 1:
            relay_in_now = relay_in.at[turn]

            @pl.when(time < group)
            def _():
                relay_in_now[...] = jnp.zeros((8, BLOCK), jnp.float32)

            @pl.when(time >= group)
            def _():
                relay_copy(turn, 0).wait_recv()

            delta = relay_in_now[...]
        delta = lax.fori_loop(early, place, pass_block, delta)
        moves[0:blocks, :] = delta[:blocks]
        table = own[...]
        for t in range(steps):
            delta = step(delta, at_step(table, t))
            moves[(t + 1) * blocks : (t + 2) * blocks, :] = delta[:blocks]
        if n_groups > 1:
            relay_out[turn] = delta

            @pl.when((place == group - 1) & (time < n_tm - 1))
            def _():
                for target in range(group):
                    relay_copy(turn, target).start()

        def moved(skip):
            return jnp.concatenate(
                [moves[pl.ds(skip * blocks + block, steps, stride=blocks), :] for block in range(blocks)], axis=1
            )

        guess = guess + moved(1)
        if turn < NEWTON - 1:
            previous = previous + moved(0)
    out[...] = guess

    @pl.when(time < n_tm - 1)
    def _():
        for away in range(n_unit):
            near_copy(away).wait_send()

    for turn in range(NEWTON):
        for away in range(1, n_unit):
            mate_copy(turn, away).wait_send()
        for away in range(1, group):
            @pl.when(place + away < group)
            def _():
                coef_copy(turn, away).wait_send()
        if n_groups > 1:
            @pl.when((place == group - 1) & (time < n_tm - 1))
            def _():
                for target in range(group):
                    relay_copy(turn, target).wait_send()


def shards(n_tm, n_unit, projections, recurrent, update_bias, candidate_bias, start_state, initial_guess):
    _, steps, _, width = projections.shape
    full = recurrent.shape[0]
    rows = steps * (width // BLOCK)
    group = min(GROUP, n_tm)
    side = 2 if width // BLOCK % 2 == 0 else 1
    vmem = pl.BlockSpec(memory_space=pltpu.VMEM)
    f32, bf16 = jnp.float32, jnp.bfloat16
    held = 8 * pl.cdiv(steps + 1, 8)
    dma = pltpu.SemaphoreType.DMA
    result = pl.pallas_call(
        functools.partial(newton_kernel, n_tm, n_unit),
        out_shape=jax.ShapeDtypeStruct((steps, width), f32),
        in_specs=[pl.BlockSpec(memory_space=pltpu.HBM)] * 6,
        out_specs=vmem,
        scratch_shapes=[
            pltpu.VMEM((3, steps, width), bf16),
            pltpu.VMEM((1, width), f32),
            pltpu.VMEM((1, width), f32),
            pltpu.VMEM((3, full, width), bf16),
            pltpu.VMEM((side * BLOCK, 3 * (width // side)), bf16),
            pltpu.VMEM((NEWTON, held, width), f32),
            pltpu.VMEM((NEWTON, n_unit - 1, held, width), f32),
            pltpu.VMEM((n_unit, held, width), f32),
            pltpu.VMEM((COEFS, rows, BLOCK), f32),
            pltpu.VMEM((NEWTON, SENT, rows, BLOCK), bf16),
            pltpu.VMEM((NEWTON, group - 1, SENT, rows, BLOCK), bf16),
            pltpu.VMEM((rows + 8, BLOCK), f32),
            pltpu.VMEM((NEWTON, 8, BLOCK), f32),
            pltpu.VMEM((NEWTON, 8, BLOCK), f32),
            dma((5,)),
            dma((3,)),
            dma((NEWTON, n_unit - 1)),
            dma((NEWTON, n_unit - 1)),
            dma((n_unit,)),
            dma((n_unit,)),
            dma((NEWTON, group - 1)),
            dma((NEWTON, group - 1)),
            dma((NEWTON, group)),
            dma((NEWTON,)),
        ],
        compiler_params=pltpu.CompilerParams(
            collective_id=0, has_side_effects=True, vmem_limit_bytes=60 * 1024 * 1024
        ),
        name="newton",
    )(
        jnp.transpose(projections[0], (1, 0, 2)),
        jnp.transpose(recurrent, (1, 0, 2)),
        update_bias.reshape(1, width),
        candidate_bias.reshape(1, width),
        start_state,
        initial_guess[0],
    )
    return result[None]


def solution(mesh):
    return jax.shard_map(
        functools.partial(shards, mesh.shape["tm"], mesh.shape["unit"]),
        mesh=mesh,
        in_specs=(
            P("sweep", "tm", None, "unit"),
            P("sweep", None, "unit"),
            P(("sweep", "unit")),
            P(("sweep", "unit")),
            P("sweep", "unit"),
            P("sweep", "tm", "unit"),
        ),
        out_specs=P("sweep", "tm", "unit"),
        check_vma=False,
    )
```

```python
import functools

import jax
import jax.numpy as jnp
from jax import lax
from jax.experimental import pallas as pl
from jax.experimental.pallas import tpu as pltpu
from jax.sharding import PartitionSpec as P

BLOCK = 128
NEWTON = 2
GROUP = 4
COEFS = 5
FINE = (0, 4)
SENT = COEFS + len(FINE)
MESH = pl.DeviceIdType.MESH


def to(tm, unit):
    return {"tm": tm, "unit": unit}


def newton_kernel(
    n_tm, n_unit, proj_hbm, w_hbm, bias_u_hbm, bias_c_hbm, start_hbm, guess_hbm, out,
    proj, bias_u, bias_c, w_all, w_diag, stage, mates, nears, own, packed, coefs, moves, relay_out, relay_in,
    in_sem, w_sem, mate_send, mate_recv, near_send, near_recv, coef_send, coef_recv, relay_send, relay_recv,
):
    steps, width = guess_hbm.shape
    blocks = width // BLOCK
    rows = steps * blocks
    side = 2 if blocks % 2 == 0 else 1
    group = min(GROUP, n_tm)
    n_groups = n_tm // group
    time = lax.axis_index("tm")
    unit = lax.axis_index("unit")
    place = lax.rem(time, group)
    reach = min(n_tm - 1, group if n_groups > 1 else group - 1)

    smalls = [
        pltpu.make_async_copy(source, target, in_sem.at[index])
        for index, (source, target) in enumerate((
            (guess_hbm, stage.at[0, pl.ds(0, steps)]),
            (start_hbm, stage.at[0, pl.ds(steps, 1)]),
            (proj_hbm, proj),
            (bias_u_hbm, bias_u),
            (bias_c_hbm, bias_c),
        ))
    ]
    for load in smalls:
        load.start()
    loads = [
        pltpu.make_async_copy(w_hbm.at[gate], w_all.at[gate], w_sem.at[gate]) for gate in range(3)
    ]
    for load in loads:
        load.start()

    barrier = pltpu.get_barrier_semaphore()
    greeted = jnp.int32(n_unit - 1)
    for away in range(1, n_unit):
        pl.semaphore_signal(
            barrier, inc=1, device_id=to(time, lax.rem(unit + away, n_unit)), device_id_type=MESH
        )
    for away in range(1, reach + 1):
        turns = range(n_unit if away == 1 else 1)
        for there, valid in ((time + away, time + away < n_tm), (time - away, time >= away)):
            greeted = greeted + jnp.where(valid, len(turns), 0)

            @pl.when(valid)
            def _():
                for turn in turns:
                    pl.semaphore_signal(
                        barrier, inc=1, device_id=to(there, lax.rem(unit + turn, n_unit)), device_id_type=MESH
                    )

    for load in smalls[:2]:
        load.wait()
    pl.semaphore_wait(barrier, greeted)

    def mate_copy(turn, away):
        return pltpu.make_async_remote_copy(
            src_ref=stage.at[turn], dst_ref=mates.at[turn, away - 1],
            send_sem=mate_send.at[turn, away - 1], recv_sem=mate_recv.at[turn, away - 1],
            device_id=to(time, lax.rem(unit + away, n_unit)), device_id_type=MESH,
        )

    def near_copy(away):
        return pltpu.make_async_remote_copy(
            src_ref=stage.at[0], dst_ref=nears.at[away],
            send_sem=near_send.at[away], recv_sem=near_recv.at[away],
            device_id=to(lax.rem(time + 1, n_tm), lax.rem(unit + away, n_unit)), device_id_type=MESH,
        )

    def coef_copy(turn, away):
        return pltpu.make_async_remote_copy(
            src_ref=packed.at[turn], dst_ref=coefs.at[turn, away - 1],
            send_sem=coef_send.at[turn, away - 1], recv_sem=coef_recv.at[turn, away - 1],
            device_id=to(lax.rem(time + away, n_tm), unit), device_id_type=MESH,
        )

    def relay_copy(turn, target):
        return pltpu.make_async_remote_copy(
            src_ref=relay_out.at[turn], dst_ref=relay_in.at[turn],
            send_sem=relay_send.at[turn, target], recv_sem=relay_recv.at[turn],
            device_id=to(lax.rem(time + 1 + target, n_tm), unit), device_id_type=MESH,
        )

    for away in range(1, n_unit):
        mate_copy(0, away).start()

    @pl.when(time < n_tm - 1)
    def _():
        for away in range(n_unit):
            near_copy(away).start()

    def gate_column(pair, gate):
        pairs = blocks // side
        return (2 * pair + gate if gate < 2 else 2 * pairs + pair) * BLOCK


    for load in loads:
        load.wait()
    for load in smalls[2:]:
        load.wait()
    for block in range(blocks):
        first = pl.multiple_of(unit * width + block * BLOCK, BLOCK)
        here = slice(block * BLOCK, (block + 1) * BLOCK)
        depth = block % side * BLOCK
        for gate in range(3):
            column = gate_column(block // side, gate)
            w_diag[depth : depth + BLOCK, column : column + BLOCK] = w_all[gate, pl.ds(first, BLOCK), here]

    @pl.when(time > 0)
    def _():
        for away in range(n_unit):
            near_copy(away).wait_recv()

    def entering_from(held, away):
        return jnp.where(time == 0, held[steps : steps + 1, :], nears[(n_unit - away) % n_unit, steps - 1 : steps, :])

    guess = stage[0, 0:steps, :]
    previous = jnp.concatenate([entering_from(stage[0], 0), guess[: steps - 1]], axis=0)
    row = lax.broadcasted_iota(jnp.int32, (8, BLOCK), 0)

    for turn in range(NEWTON):
        if turn:
            stage[turn, 0:steps, :] = previous
            for away in range(1, n_unit):
                mate_copy(turn, away).start()

        def product(panel, owner):
            first = pl.multiple_of(owner * width, width)
            panel = jnp.concatenate([panel] * (16 // steps), axis=0).astype(jnp.bfloat16)
            return [
                jnp.dot(panel, w_all[gate, pl.ds(first, width), :], preferred_element_type=jnp.float32)[:steps]
                for gate in range(3)
            ]

        def step(delta, five):
            left = jnp.concatenate(
                [jnp.where((row % side == depth) & (row < blocks), delta, 0.0) for depth in range(side)], axis=1
            ).astype(jnp.bfloat16)
            terms = jnp.dot(left, w_diag[...], preferred_element_type=jnp.float32)

            def of_gate(gate):
                value = None
                for pair in range(blocks // side):
                    column = gate_column(pair, gate)
                    part = terms[:, column : column + BLOCK]
                    value = part if value is None else jnp.where(row // side == pair, part, value)
                return value

            fresh, a, c, d, gap = five
            return (
                (gap + delta - fresh * delta) + a * of_gate(0) + c * of_gate(1) + d * of_gate(2)
            )

        def at_step(table, t):
            def pick(value):
                part = value[t * blocks : (t + 1) * blocks]
                return jnp.concatenate([part] * (8 // blocks), axis=0)

            return [pick(table[index]) for index in range(COEFS)]

        def pass_block(source, delta):
            away = place - source
            slot = away - 1
            pltpu.make_async_remote_copy(
                src_ref=packed.at[turn], dst_ref=coefs.at[turn, slot],
                send_sem=coef_send.at[turn, slot], recv_sem=coef_recv.at[turn, slot],
                device_id=to(lax.rem(time + 1, n_tm), unit), device_id_type=MESH,
            ).wait_recv()
            table = [coefs[turn, slot, index].astype(jnp.float32) for index in range(SENT)]
            for low, index in enumerate(FINE):
                table[index] = table[index] + table[COEFS + low]
            for t in range(steps):
                delta = step(delta, at_step(table, t))
            return delta

        rec = product(previous, unit)
        early = jnp.int32(0)
        if turn == 0 or n_groups > 1:
            delta = jnp.zeros((8, BLOCK), jnp.float32)
        else:
            early = (2 * place) // group
            delta = lax.fori_loop(0, early, pass_block, jnp.zeros((8, BLOCK), jnp.float32))
        for away in range(1, n_unit):
            mate_copy(turn, away).wait_recv()
            held = mates[turn, away - 1]
            if turn:
                panel = held[:steps]
            else:
                panel = jnp.concatenate([entering_from(held, n_unit - away), held[: steps - 1]], axis=0)
            rec = [x + y for x, y in zip(rec, product(panel, lax.rem(unit + n_unit - away, n_unit)))]

        update_in = proj[0].astype(jnp.float32) + rec[0] + bias_u[...]
        update = jax.nn.sigmoid(update_in)
        fresh = jax.nn.sigmoid(-update_in)
        reset = jax.nn.sigmoid(proj[1].astype(jnp.float32) + rec[1])
        cand_rec = rec[2] + bias_c[...]
        cand = jnp.tanh(proj[2].astype(jnp.float32) + reset * cand_rec)
        coef_d = fresh * (1.0 - cand * cand) * reset
        values = (
            fresh,
            (previous - cand) * update * fresh,
            coef_d * cand_rec * (1.0 - reset),
            coef_d,
            fresh * cand + update * previous - guess,
        )
        for index, value in enumerate(values):
            for block in range(blocks):
                own[index, pl.ds(block, steps, stride=blocks), :] = value[:, block * BLOCK : (block + 1) * BLOCK]
        packed[turn, 0:COEFS] = own[...].astype(jnp.bfloat16)
        for slot, index in enumerate(FINE):
            full = own[index]
            packed[turn, COEFS + slot] = (full - full.astype(jnp.bfloat16).astype(jnp.float32)).astype(jnp.bfloat16)

        for away in range(group - 1, 0, -1):
            @pl.when(place + away < group)
            def _():
                coef_copy(turn, away).start()

        if n_groups > 1:
            relay_in_now = relay_in.at[turn]

            @pl.when(time < group)
            def _():
                relay_in_now[...] = jnp.zeros((8, BLOCK), jnp.float32)

            @pl.when(time >= group)
            def _():
                relay_copy(turn, 0).wait_recv()

            delta = relay_in_now[...]
        delta = lax.fori_loop(early, place, pass_block, delta)
        moves[0:blocks, :] = delta[:blocks]
        table = own[...]
        for t in range(steps):
            delta = step(delta, at_step(table, t))
            moves[(t + 1) * blocks : (t + 2) * blocks, :] = delta[:blocks]
        if n_groups > 1:
            relay_out[turn] = delta

            @pl.when((place == group - 1) & (time < n_tm - 1))
            def _():
                for target in reversed(range(group)):
                    relay_copy(turn, target).start()

        def moved(skip):
            return jnp.concatenate(
                [moves[pl.ds(skip * blocks + block, steps, stride=blocks), :] for block in range(blocks)], axis=1
            )

        guess = guess + moved(1)
        if turn < NEWTON - 1:
            previous = previous + moved(0)
    out[...] = guess

    @pl.when(time < n_tm - 1)
    def _():
        for away in range(n_unit):
            near_copy(away).wait_send()

    for turn in range(NEWTON):
        for away in range(1, n_unit):
            mate_copy(turn, away).wait_send()
        for away in range(1, group):
            @pl.when(place + away < group)
            def _():
                coef_copy(turn, away).wait_send()
        if n_groups > 1:
            @pl.when((place == group - 1) & (time < n_tm - 1))
            def _():
                for target in range(group):
                    relay_copy(turn, target).wait_send()


def shards(n_tm, n_unit, projections, recurrent, update_bias, candidate_bias, start_state, initial_guess):
    _, steps, _, width = projections.shape
    full = recurrent.shape[0]
    rows = steps * (width // BLOCK)
    group = min(GROUP, n_tm)
    side = 2 if width // BLOCK % 2 == 0 else 1
    vmem = pl.BlockSpec(memory_space=pltpu.VMEM)
    f32, bf16 = jnp.float32, jnp.bfloat16
    held = 8 * pl.cdiv(steps + 1, 8)
    dma = pltpu.SemaphoreType.DMA
    result = pl.pallas_call(
        functools.partial(newton_kernel, n_tm, n_unit),
        out_shape=jax.ShapeDtypeStruct((steps, width), f32),
        in_specs=[pl.BlockSpec(memory_space=pltpu.HBM)] * 6,
        out_specs=vmem,
        scratch_shapes=[
            pltpu.VMEM((3, steps, width), bf16),
            pltpu.VMEM((1, width), f32),
            pltpu.VMEM((1, width), f32),
            pltpu.VMEM((3, full, width), bf16),
            pltpu.VMEM((side * BLOCK, 3 * (width // side)), bf16),
            pltpu.VMEM((NEWTON, held, width), f32),
            pltpu.VMEM((NEWTON, n_unit - 1, held, width), f32),
            pltpu.VMEM((n_unit, held, width), f32),
            pltpu.VMEM((COEFS, rows, BLOCK), f32),
            pltpu.VMEM((NEWTON, SENT, rows, BLOCK), bf16),
            pltpu.VMEM((NEWTON, group - 1, SENT, rows, BLOCK), bf16),
            pltpu.VMEM((rows + 8, BLOCK), f32),
            pltpu.VMEM((NEWTON, 8, BLOCK), f32),
            pltpu.VMEM((NEWTON, 8, BLOCK), f32),
            dma((5,)),
            dma((3,)),
            dma((NEWTON, n_unit - 1)),
            dma((NEWTON, n_unit - 1)),
            dma((n_unit,)),
            dma((n_unit,)),
            dma((NEWTON, group - 1)),
            dma((NEWTON, group - 1)),
            dma((NEWTON, group)),
            dma((NEWTON,)),
        ],
        compiler_params=pltpu.CompilerParams(
            collective_id=0, has_side_effects=True, vmem_limit_bytes=60 * 1024 * 1024
        ),
        name="newton",
    )(
        jnp.transpose(projections[0], (1, 0, 2)),
        jnp.transpose(recurrent, (1, 0, 2)),
        update_bias.reshape(1, width),
        candidate_bias.reshape(1, width),
        start_state,
        initial_guess[0],
    )
    return result[None]


def solution(mesh):
    return jax.shard_map(
        functools.partial(shards, mesh.shape["tm"], mesh.shape["unit"]),
        mesh=mesh,
        in_specs=(
            P("sweep", "tm", None, "unit"),
            P("sweep", None, "unit"),
            P(("sweep", "unit")),
            P(("sweep", "unit")),
            P("sweep", "unit"),
            P("sweep", "tm", "unit"),
        ),
        out_specs=P("sweep", "tm", "unit"),
        check_vma=False,
    )
```

```python
import functools

import jax
import jax.numpy as jnp
from jax import lax
from jax.experimental import pallas as pl
from jax.experimental.pallas import tpu as pltpu
from jax.sharding import PartitionSpec as P

BLOCK = 128
NEWTON = 2
GROUP = 4
COEFS = 5
FINE = (0, 4)
SENT = COEFS + len(FINE)
MESH = pl.DeviceIdType.MESH


def to(tm, unit):
    return {"tm": tm, "unit": unit}


def newton_kernel(
    n_tm, n_unit, proj_hbm, w_hbm, bias_u_hbm, bias_c_hbm, start_hbm, guess_hbm, out,
    proj, bias_u, bias_c, w_all, w_diag, stage, mates, nears, own, packed, coefs, ready, moves, relay_out, relay_in,
    in_sem, w_sem, mate_send, mate_recv, near_send, near_recv, coef_send, coef_recv, relay_send, relay_recv,
):
    steps, width = guess_hbm.shape
    blocks = width // BLOCK
    rows = steps * blocks
    side = 2 if blocks % 2 == 0 else 1
    group = min(GROUP, n_tm)
    n_groups = n_tm // group
    time = lax.axis_index("tm")
    unit = lax.axis_index("unit")
    place = lax.rem(time, group)
    reach = min(n_tm - 1, group if n_groups > 1 else group - 1)

    smalls = [
        pltpu.make_async_copy(source, target, in_sem.at[index])
        for index, (source, target) in enumerate((
            (guess_hbm, stage.at[0, pl.ds(0, steps)]),
            (start_hbm, stage.at[0, pl.ds(steps, 1)]),
            (proj_hbm, proj),
            (bias_u_hbm, bias_u),
            (bias_c_hbm, bias_c),
        ))
    ]
    for load in smalls:
        load.start()
    loads = [
        pltpu.make_async_copy(w_hbm.at[gate], w_all.at[gate], w_sem.at[gate]) for gate in range(3)
    ]
    for load in loads:
        load.start()

    ready[...] = jnp.zeros(ready.shape, jnp.float32)
    barrier = pltpu.get_barrier_semaphore()
    greeted = jnp.int32(n_unit - 1)
    for away in range(1, n_unit):
        pl.semaphore_signal(
            barrier, inc=1, device_id=to(time, lax.rem(unit + away, n_unit)), device_id_type=MESH
        )
    for away in range(1, reach + 1):
        turns = range(n_unit if away == 1 else 1)
        for there, valid in ((time + away, time + away < n_tm), (time - away, time >= away)):
            greeted = greeted + jnp.where(valid, len(turns), 0)

            @pl.when(valid)
            def _():
                for turn in turns:
                    pl.semaphore_signal(
                        barrier, inc=1, device_id=to(there, lax.rem(unit + turn, n_unit)), device_id_type=MESH
                    )

    for load in smalls[:2]:
        load.wait()
    pl.semaphore_wait(barrier, greeted)

    def mate_copy(turn, away):
        return pltpu.make_async_remote_copy(
            src_ref=stage.at[turn], dst_ref=mates.at[turn, away - 1],
            send_sem=mate_send.at[turn, away - 1], recv_sem=mate_recv.at[turn, away - 1],
            device_id=to(time, lax.rem(unit + away, n_unit)), device_id_type=MESH,
        )

    def near_copy(away):
        return pltpu.make_async_remote_copy(
            src_ref=stage.at[0], dst_ref=nears.at[away],
            send_sem=near_send.at[away], recv_sem=near_recv.at[away],
            device_id=to(lax.rem(time + 1, n_tm), lax.rem(unit + away, n_unit)), device_id_type=MESH,
        )

    def coef_copy(turn, away):
        return pltpu.make_async_remote_copy(
            src_ref=packed.at[turn], dst_ref=coefs.at[turn, away - 1],
            send_sem=coef_send.at[turn, away - 1], recv_sem=coef_recv.at[turn, away - 1],
            device_id=to(lax.rem(time + away, n_tm), unit), device_id_type=MESH,
        )

    def relay_copy(turn, target):
        return pltpu.make_async_remote_copy(
            src_ref=relay_out.at[turn], dst_ref=relay_in.at[turn],
            send_sem=relay_send.at[turn, target], recv_sem=relay_recv.at[turn],
            device_id=to(lax.rem(time + 1 + target, n_tm), unit), device_id_type=MESH,
        )

    for away in range(1, n_unit):
        mate_copy(0, away).start()

    @pl.when(time < n_tm - 1)
    def _():
        for away in range(n_unit):
            near_copy(away).start()

    def gate_column(pair, gate):
        pairs = blocks // side
        return (2 * pair + gate if gate < 2 else 2 * pairs + pair) * BLOCK


    for load in loads:
        load.wait()
    for load in smalls[2:]:
        load.wait()
    for block in range(blocks):
        first = pl.multiple_of(unit * width + block * BLOCK, BLOCK)
        here = slice(block * BLOCK, (block + 1) * BLOCK)
        depth = block % side * BLOCK
        for gate in range(3):
            column = gate_column(block // side, gate)
            w_diag[depth : depth + BLOCK, column : column + BLOCK] = w_all[gate, pl.ds(first, BLOCK), here]

    @pl.when(time > 0)
    def _():
        for away in range(n_unit):
            near_copy(away).wait_recv()

    def entering_from(held, away):
        return jnp.where(time == 0, held[steps : steps + 1, :], nears[(n_unit - away) % n_unit, steps - 1 : steps, :])

    guess = stage[0, 0:steps, :]
    previous = jnp.concatenate([entering_from(stage[0], 0), guess[: steps - 1]], axis=0)
    row = lax.broadcasted_iota(jnp.int32, (8, BLOCK), 0)

    for turn in range(NEWTON):
        if turn:
            stage[turn, 0:steps, :] = previous
            for away in range(1, n_unit):
                mate_copy(turn, away).start()

        def product(panel, owner):
            first = pl.multiple_of(owner * width, width)
            panel = jnp.concatenate([panel] * (16 // steps), axis=0).astype(jnp.bfloat16)
            return [
                jnp.dot(panel, w_all[gate, pl.ds(first, width), :], preferred_element_type=jnp.float32)[:steps]
                for gate in range(3)
            ]

        def step(delta, five):
            left = jnp.concatenate(
                [jnp.where((row % side == depth) & (row < blocks), delta, 0.0) for depth in range(side)], axis=1
            ).astype(jnp.bfloat16)
            terms = jnp.dot(left, w_diag[...], preferred_element_type=jnp.float32)

            def of_gate(gate):
                value = None
                for pair in range(blocks // side):
                    column = gate_column(pair, gate)
                    part = terms[:, column : column + BLOCK]
                    value = part if value is None else jnp.where(row // side == pair, part, value)
                return value

            fresh, a, c, d, gap = five
            return (
                (gap + delta - fresh * delta) + a * of_gate(0) + c * of_gate(1) + d * of_gate(2)
            )

        def spread(slot, table):
            for index in range(COEFS):
                for t in range(steps):
                    ready[slot, index, t, 0:blocks, :] = table[index][t * blocks : (t + 1) * blocks]

        def prepare(source):
            slot = place - source - 1
            pltpu.make_async_remote_copy(
                src_ref=packed.at[turn], dst_ref=coefs.at[turn, slot],
                send_sem=coef_send.at[turn, slot], recv_sem=coef_recv.at[turn, slot],
                device_id=to(lax.rem(time + 1, n_tm), unit), device_id_type=MESH,
            ).wait_recv()
            table = [coefs[turn, slot, index].astype(jnp.float32) for index in range(SENT)]
            for low, index in enumerate(FINE):
                table[index] = table[index] + table[COEFS + low]
            spread(slot, table)

        def prepare_ahead(source, carry):
            prepare(source)
            return carry

        def at_step(slot, t):
            return [ready[slot, index, t] for index in range(COEFS)]

        def pass_block(source, delta):
            @pl.when(source >= ahead)
            def _():
                prepare(source)

            for t in range(steps):
                delta = step(delta, at_step(place - source - 1, t))
            return delta

        rec = product(previous, unit)
        for away in range(1, n_unit):
            mate_copy(turn, away).wait_recv()
            held = mates[turn, away - 1]
            if turn:
                panel = held[:steps]
            else:
                panel = jnp.concatenate([entering_from(held, n_unit - away), held[: steps - 1]], axis=0)
            rec = [x + y for x, y in zip(rec, product(panel, lax.rem(unit + n_unit - away, n_unit)))]

        update_in = proj[0].astype(jnp.float32) + rec[0] + bias_u[...]
        update = jax.nn.sigmoid(update_in)
        fresh = jax.nn.sigmoid(-update_in)
        reset = jax.nn.sigmoid(proj[1].astype(jnp.float32) + rec[1])
        cand_rec = rec[2] + bias_c[...]
        cand = jnp.tanh(proj[2].astype(jnp.float32) + reset * cand_rec)
        coef_d = fresh * (1.0 - cand * cand) * reset
        values = (
            fresh,
            (previous - cand) * update * fresh,
            coef_d * cand_rec * (1.0 - reset),
            coef_d,
            fresh * cand + update * previous - guess,
        )
        for index, value in enumerate(values):
            for block in range(blocks):
                own[index, pl.ds(block, steps, stride=blocks), :] = value[:, block * BLOCK : (block + 1) * BLOCK]
        packed[turn, 0:COEFS] = own[...].astype(jnp.bfloat16)
        for slot, index in enumerate(FINE):
            full = own[index]
            packed[turn, COEFS + slot] = (full - full.astype(jnp.bfloat16).astype(jnp.float32)).astype(jnp.bfloat16)

        for away in range(group - 1, 0, -1):
            @pl.when(place + away < group)
            def _():
                coef_copy(turn, away).start()

        spread(group - 1, [own[index] for index in range(COEFS)])
        ahead = jnp.where(time < group, 0, jnp.maximum(place - turn, 0))
        lax.fori_loop(0, ahead, prepare_ahead, 0)
        delta = jnp.zeros((8, BLOCK), jnp.float32)
        if n_groups > 1:
            relay_in_now = relay_in.at[turn]

            @pl.when(time < group)
            def _():
                relay_in_now[...] = jnp.zeros((8, BLOCK), jnp.float32)

            @pl.when(time >= group)
            def _():
                relay_copy(turn, 0).wait_recv()

            delta = relay_in_now[...]
        delta = lax.fori_loop(0, place, pass_block, delta)
        moves[0:blocks, :] = delta[:blocks]
        for t in range(steps):
            delta = step(delta, at_step(group - 1, t))
            moves[(t + 1) * blocks : (t + 2) * blocks, :] = delta[:blocks]
        if n_groups > 1:
            relay_out[turn] = delta

            @pl.when((place == group - 1) & (time < n_tm - 1))
            def _():
                for target in reversed(range(group)):
                    relay_copy(turn, target).start()

        def moved(skip):
            return jnp.concatenate(
                [moves[pl.ds(skip * blocks + block, steps, stride=blocks), :] for block in range(blocks)], axis=1
            )

        guess = guess + moved(1)
        if turn < NEWTON - 1:
            previous = previous + moved(0)
    out[...] = guess

    @pl.when(time < n_tm - 1)
    def _():
        for away in range(n_unit):
            near_copy(away).wait_send()

    for turn in range(NEWTON):
        for away in range(1, n_unit):
            mate_copy(turn, away).wait_send()
        for away in range(1, group):
            @pl.when(place + away < group)
            def _():
                coef_copy(turn, away).wait_send()
        if n_groups > 1:
            @pl.when((place == group - 1) & (time < n_tm - 1))
            def _():
                for target in range(group):
                    relay_copy(turn, target).wait_send()


def shards(n_tm, n_unit, projections, recurrent, update_bias, candidate_bias, start_state, initial_guess):
    _, steps, _, width = projections.shape
    full = recurrent.shape[0]
    rows = steps * (width // BLOCK)
    group = min(GROUP, n_tm)
    side = 2 if width // BLOCK % 2 == 0 else 1
    vmem = pl.BlockSpec(memory_space=pltpu.VMEM)
    f32, bf16 = jnp.float32, jnp.bfloat16
    held = 8 * pl.cdiv(steps + 1, 8)
    dma = pltpu.SemaphoreType.DMA
    result = pl.pallas_call(
        functools.partial(newton_kernel, n_tm, n_unit),
        out_shape=jax.ShapeDtypeStruct((steps, width), f32),
        in_specs=[pl.BlockSpec(memory_space=pltpu.HBM)] * 6,
        out_specs=vmem,
        scratch_shapes=[
            pltpu.VMEM((3, steps, width), bf16),
            pltpu.VMEM((1, width), f32),
            pltpu.VMEM((1, width), f32),
            pltpu.VMEM((3, full, width), bf16),
            pltpu.VMEM((side * BLOCK, 3 * (width // side)), bf16),
            pltpu.VMEM((NEWTON, held, width), f32),
            pltpu.VMEM((NEWTON, n_unit - 1, held, width), f32),
            pltpu.VMEM((n_unit, held, width), f32),
            pltpu.VMEM((COEFS, rows, BLOCK), f32),
            pltpu.VMEM((NEWTON, SENT, rows, BLOCK), bf16),
            pltpu.VMEM((NEWTON, group - 1, SENT, rows, BLOCK), bf16),
            pltpu.VMEM((group, COEFS, steps, 8, BLOCK), f32),
            pltpu.VMEM((rows + 8, BLOCK), f32),
            pltpu.VMEM((NEWTON, 8, BLOCK), f32),
            pltpu.VMEM((NEWTON, 8, BLOCK), f32),
            dma((5,)),
            dma((3,)),
            dma((NEWTON, n_unit - 1)),
            dma((NEWTON, n_unit - 1)),
            dma((n_unit,)),
            dma((n_unit,)),
            dma((NEWTON, group - 1)),
            dma((NEWTON, group - 1)),
            dma((NEWTON, group)),
            dma((NEWTON,)),
        ],
        compiler_params=pltpu.CompilerParams(
            collective_id=0, has_side_effects=True, vmem_limit_bytes=60 * 1024 * 1024
        ),
        name="newton",
    )(
        jnp.transpose(projections[0], (1, 0, 2)),
        jnp.transpose(recurrent, (1, 0, 2)),
        update_bias.reshape(1, width),
        candidate_bias.reshape(1, width),
        start_state,
        initial_guess[0],
    )
    return result[None]


def solution(mesh):
    return jax.shard_map(
        functools.partial(shards, mesh.shape["tm"], mesh.shape["unit"]),
        mesh=mesh,
        in_specs=(
            P("sweep", "tm", None, "unit"),
            P("sweep", None, "unit"),
            P(("sweep", "unit")),
            P(("sweep", "unit")),
            P("sweep", "unit"),
            P("sweep", "tm", "unit"),
        ),
        out_specs=P("sweep", "tm", "unit"),
        check_vma=False,
    )
```

```python
import functools

import jax
import jax.numpy as jnp
from jax import lax
from jax.experimental import pallas as pl
from jax.experimental.pallas import tpu as pltpu
from jax.sharding import PartitionSpec as P

BLOCK = 128
NEWTON = 2
GROUP = 4
COEFS = 5
FINE = (0, 4)
SENT = COEFS + len(FINE)
MESH = pl.DeviceIdType.MESH


def to(tm, unit):
    return {"tm": tm, "unit": unit}


def newton_kernel(
    n_tm, n_unit, proj_hbm, w_hbm, bias_u_hbm, bias_c_hbm, start_hbm, guess_hbm, out,
    proj, bias_u, bias_c, w_all, w_diag, stage, mates, nears, own, packed, coefs, moves, relay_out, relay_in,
    in_sem, w_sem, mate_send, mate_recv, near_send, near_recv, coef_send, coef_recv, relay_send, relay_recv,
):
    steps, width = guess_hbm.shape
    blocks = width // BLOCK
    rows = steps * blocks
    side = 2 if blocks % 2 == 0 else 1
    group = min(GROUP, n_tm)
    n_groups = n_tm // group
    time = lax.axis_index("tm")
    unit = lax.axis_index("unit")
    place = lax.rem(time, group)
    reach = min(n_tm - 1, group if n_groups > 1 else group - 1)

    smalls = [
        pltpu.make_async_copy(source, target, in_sem.at[index])
        for index, (source, target) in enumerate((
            (guess_hbm, stage.at[0, pl.ds(0, steps)]),
            (start_hbm, stage.at[0, pl.ds(steps, 1)]),
            (proj_hbm, proj),
            (bias_u_hbm, bias_u),
            (bias_c_hbm, bias_c),
        ))
    ]
    for load in smalls:
        load.start()
    loads = [
        pltpu.make_async_copy(w_hbm.at[gate], w_all.at[gate], w_sem.at[gate]) for gate in range(3)
    ]
    for load in loads:
        load.start()

    barrier = pltpu.get_barrier_semaphore()
    greeted = jnp.int32(n_unit - 1)
    for away in range(1, n_unit):
        pl.semaphore_signal(
            barrier, inc=1, device_id=to(time, lax.rem(unit + away, n_unit)), device_id_type=MESH
        )
    for away in range(1, reach + 1):
        turns = range(n_unit if away == 1 else 1)
        for there, valid in ((time + away, time + away < n_tm), (time - away, time >= away)):
            greeted = greeted + jnp.where(valid, len(turns), 0)

            @pl.when(valid)
            def _():
                for turn in turns:
                    pl.semaphore_signal(
                        barrier, inc=1, device_id=to(there, lax.rem(unit + turn, n_unit)), device_id_type=MESH
                    )

    for load in smalls[:2]:
        load.wait()
    pl.semaphore_wait(barrier, greeted)

    def mate_copy(turn, away):
        return pltpu.make_async_remote_copy(
            src_ref=stage.at[turn], dst_ref=mates.at[turn, away - 1],
            send_sem=mate_send.at[turn, away - 1], recv_sem=mate_recv.at[turn, away - 1],
            device_id=to(time, lax.rem(unit + away, n_unit)), device_id_type=MESH,
        )

    def near_copy(away):
        return pltpu.make_async_remote_copy(
            src_ref=stage.at[0], dst_ref=nears.at[away],
            send_sem=near_send.at[away], recv_sem=near_recv.at[away],
            device_id=to(lax.rem(time + 1, n_tm), lax.rem(unit + away, n_unit)), device_id_type=MESH,
        )

    def coef_copy(turn, away):
        return pltpu.make_async_remote_copy(
            src_ref=packed.at[turn], dst_ref=coefs.at[turn, away - 1],
            send_sem=coef_send.at[turn, away - 1], recv_sem=coef_recv.at[turn, away - 1],
            device_id=to(lax.rem(time + away, n_tm), unit), device_id_type=MESH,
        )

    def relay_copy(turn, target):
        return pltpu.make_async_remote_copy(
            src_ref=relay_out.at[turn], dst_ref=relay_in.at[turn],
            send_sem=relay_send.at[turn, target], recv_sem=relay_recv.at[turn],
            device_id=to(lax.rem(time + 1 + target, n_tm), unit), device_id_type=MESH,
        )

    for away in range(1, n_unit):
        mate_copy(0, away).start()

    @pl.when(time < n_tm - 1)
    def _():
        for away in range(n_unit):
            near_copy(away).start()

    def gate_column(pair, gate):
        pairs = blocks // side
        return (2 * pair + gate if gate < 2 else 2 * pairs + pair) * BLOCK


    for load in loads:
        load.wait()
    for load in smalls[2:]:
        load.wait()
    for block in range(blocks):
        first = pl.multiple_of(unit * width + block * BLOCK, BLOCK)
        here = slice(block * BLOCK, (block + 1) * BLOCK)
        depth = block % side * BLOCK
        for gate in range(3):
            column = gate_column(block // side, gate)
            w_diag[depth : depth + BLOCK, column : column + BLOCK] = w_all[gate, pl.ds(first, BLOCK), here]

    @pl.when(time > 0)
    def _():
        for away in range(n_unit):
            near_copy(away).wait_recv()

    def entering_from(held, away):
        return jnp.where(time == 0, held[steps : steps + 1, :], nears[(n_unit - away) % n_unit, steps - 1 : steps, :])

    guess = stage[0, 0:steps, :]
    previous = jnp.concatenate([entering_from(stage[0], 0), guess[: steps - 1]], axis=0)
    row = lax.broadcasted_iota(jnp.int32, (8, BLOCK), 0)

    for turn in range(NEWTON):
        if turn:
            stage[turn, 0:steps, :] = previous
            for away in range(1, n_unit):
                mate_copy(turn, away).start()

        def product(panel, owner):
            first = pl.multiple_of(owner * width, width)
            panel = jnp.concatenate([panel] * (16 // steps), axis=0).astype(jnp.bfloat16)
            return [
                jnp.dot(panel, w_all[gate, pl.ds(first, width), :], preferred_element_type=jnp.float32)[:steps]
                for gate in range(3)
            ]

        def step(delta, five):
            left = jnp.concatenate(
                [jnp.where((row % side == depth) & (row < blocks), delta, 0.0) for depth in range(side)], axis=1
            ).astype(jnp.bfloat16)

            def of_gate(gate):
                value = None
                for pair in range(blocks // side):
                    column = gate_column(pair, gate)
                    part = jnp.dot(left, w_diag[:, column : column + BLOCK], preferred_element_type=jnp.float32)
                    value = part if value is None else jnp.where(row // side == pair, part, value)
                return value

            fresh, a, c, d, gap = five
            return (
                (gap + delta - fresh * delta) + a * of_gate(0) + c * of_gate(1) + d * of_gate(2)
            )

        def at_step(table, t):
            def pick(value):
                part = value[t * blocks : (t + 1) * blocks]
                return jnp.concatenate([part] * (8 // blocks), axis=0)

            return [pick(table[index]) for index in range(COEFS)]

        def pass_block(source, delta):
            away = place - source
            slot = away - 1
            pltpu.make_async_remote_copy(
                src_ref=packed.at[turn], dst_ref=coefs.at[turn, slot],
                send_sem=coef_send.at[turn, slot], recv_sem=coef_recv.at[turn, slot],
                device_id=to(lax.rem(time + 1, n_tm), unit), device_id_type=MESH,
            ).wait_recv()
            table = [coefs[turn, slot, index].astype(jnp.float32) for index in range(SENT)]
            for low, index in enumerate(FINE):
                table[index] = table[index] + table[COEFS + low]
            for t in range(steps):
                delta = step(delta, at_step(table, t))
            return delta

        rec = product(previous, unit)
        early = jnp.int32(0)
        if turn == 0 or n_groups > 1:
            delta = jnp.zeros((8, BLOCK), jnp.float32)
        else:
            early = (2 * place) // group
            delta = lax.fori_loop(0, early, pass_block, jnp.zeros((8, BLOCK), jnp.float32))
        for away in range(1, n_unit):
            mate_copy(turn, away).wait_recv()
            held = mates[turn, away - 1]
            if turn:
                panel = held[:steps]
            else:
                panel = jnp.concatenate([entering_from(held, n_unit - away), held[: steps - 1]], axis=0)
            rec = [x + y for x, y in zip(rec, product(panel, lax.rem(unit + n_unit - away, n_unit)))]

        update_in = proj[0].astype(jnp.float32) + rec[0] + bias_u[...]
        update = jax.nn.sigmoid(update_in)
        fresh = jax.nn.sigmoid(-update_in)
        reset = jax.nn.sigmoid(proj[1].astype(jnp.float32) + rec[1])
        cand_rec = rec[2] + bias_c[...]
        cand = jnp.tanh(proj[2].astype(jnp.float32) + reset * cand_rec)
        coef_d = fresh * (1.0 - cand * cand) * reset
        values = (
            fresh,
            (previous - cand) * update * fresh,
            coef_d * cand_rec * (1.0 - reset),
            coef_d,
            fresh * cand + update * previous - guess,
        )
        for index, value in enumerate(values):
            for block in range(blocks):
                own[index, pl.ds(block, steps, stride=blocks), :] = value[:, block * BLOCK : (block + 1) * BLOCK]
        packed[turn, 0:COEFS] = own[...].astype(jnp.bfloat16)
        for slot, index in enumerate(FINE):
            full = own[index]
            packed[turn, COEFS + slot] = (full - full.astype(jnp.bfloat16).astype(jnp.float32)).astype(jnp.bfloat16)

        for away in range(group - 1, 0, -1):
            @pl.when(place + away < group)
            def _():
                coef_copy(turn, away).start()

        if n_groups > 1:
            relay_in_now = relay_in.at[turn]

            @pl.when(time < group)
            def _():
                relay_in_now[...] = jnp.zeros((8, BLOCK), jnp.float32)

            @pl.when(time >= group)
            def _():
                relay_copy(turn, 0).wait_recv()

            delta = relay_in_now[...]
        delta = lax.fori_loop(early, place, pass_block, delta)
        moves[0:blocks, :] = delta[:blocks]
        table = own[...]
        for t in range(steps):
            delta = step(delta, at_step(table, t))
            moves[(t + 1) * blocks : (t + 2) * blocks, :] = delta[:blocks]
        if n_groups > 1:
            relay_out[turn] = delta

            @pl.when((place == group - 1) & (time < n_tm - 1))
            def _():
                for target in reversed(range(group)):
                    relay_copy(turn, target).start()

        def moved(skip):
            return jnp.concatenate(
                [moves[pl.ds(skip * blocks + block, steps, stride=blocks), :] for block in range(blocks)], axis=1
            )

        guess = guess + moved(1)
        if turn < NEWTON - 1:
            previous = previous + moved(0)
    out[...] = guess

    @pl.when(time < n_tm - 1)
    def _():
        for away in range(n_unit):
            near_copy(away).wait_send()

    for turn in range(NEWTON):
        for away in range(1, n_unit):
            mate_copy(turn, away).wait_send()
        for away in range(1, group):
            @pl.when(place + away < group)
            def _():
                coef_copy(turn, away).wait_send()
        if n_groups > 1:
            @pl.when((place == group - 1) & (time < n_tm - 1))
            def _():
                for target in range(group):
                    relay_copy(turn, target).wait_send()


def shards(n_tm, n_unit, projections, recurrent, update_bias, candidate_bias, start_state, initial_guess):
    _, steps, _, width = projections.shape
    full = recurrent.shape[0]
    rows = steps * (width // BLOCK)
    group = min(GROUP, n_tm)
    side = 2 if width // BLOCK % 2 == 0 else 1
    vmem = pl.BlockSpec(memory_space=pltpu.VMEM)
    f32, bf16 = jnp.float32, jnp.bfloat16
    held = 8 * pl.cdiv(steps + 1, 8)
    dma = pltpu.SemaphoreType.DMA
    result = pl.pallas_call(
        functools.partial(newton_kernel, n_tm, n_unit),
        out_shape=jax.ShapeDtypeStruct((steps, width), f32),
        in_specs=[pl.BlockSpec(memory_space=pltpu.HBM)] * 6,
        out_specs=vmem,
        scratch_shapes=[
            pltpu.VMEM((3, steps, width), bf16),
            pltpu.VMEM((1, width), f32),
            pltpu.VMEM((1, width), f32),
            pltpu.VMEM((3, full, width), bf16),
            pltpu.VMEM((side * BLOCK, 3 * (width // side)), bf16),
            pltpu.VMEM((NEWTON, held, width), f32),
            pltpu.VMEM((NEWTON, n_unit - 1, held, width), f32),
            pltpu.VMEM((n_unit, held, width), f32),
            pltpu.VMEM((COEFS, rows, BLOCK), f32),
            pltpu.VMEM((NEWTON, SENT, rows, BLOCK), bf16),
            pltpu.VMEM((NEWTON, group - 1, SENT, rows, BLOCK), bf16),
            pltpu.VMEM((rows + 8, BLOCK), f32),
            pltpu.VMEM((NEWTON, 8, BLOCK), f32),
            pltpu.VMEM((NEWTON, 8, BLOCK), f32),
            dma((5,)),
            dma((3,)),
            dma((NEWTON, n_unit - 1)),
            dma((NEWTON, n_unit - 1)),
            dma((n_unit,)),
            dma((n_unit,)),
            dma((NEWTON, group - 1)),
            dma((NEWTON, group - 1)),
            dma((NEWTON, group)),
            dma((NEWTON,)),
        ],
        compiler_params=pltpu.CompilerParams(
            collective_id=0, has_side_effects=True, vmem_limit_bytes=60 * 1024 * 1024
        ),
        name="newton",
    )(
        jnp.transpose(projections[0], (1, 0, 2)),
        jnp.transpose(recurrent, (1, 0, 2)),
        update_bias.reshape(1, width),
        candidate_bias.reshape(1, width),
        start_state,
        initial_guess[0],
    )
    return result[None]


def solution(mesh):
    return jax.shard_map(
        functools.partial(shards, mesh.shape["tm"], mesh.shape["unit"]),
        mesh=mesh,
        in_specs=(
            P("sweep", "tm", None, "unit"),
            P("sweep", None, "unit"),
            P(("sweep", "unit")),
            P(("sweep", "unit")),
            P("sweep", "unit"),
            P("sweep", "tm", "unit"),
        ),
        out_specs=P("sweep", "tm", "unit"),
        check_vma=False,
    )
```

```python
import functools

import jax
import jax.numpy as jnp
from jax import lax
from jax.experimental import pallas as pl
from jax.experimental.pallas import tpu as pltpu
from jax.sharding import PartitionSpec as P

BLOCK = 128
NEWTON = 2
GROUP = 4
COEFS = 5
FINE = (0, 4)
SENT = COEFS + len(FINE)
MESH = pl.DeviceIdType.MESH


def to(tm, unit):
    return {"tm": tm, "unit": unit}


def newton_kernel(
    n_tm, n_unit, proj_hbm, w_hbm, bias_u_hbm, bias_c_hbm, start_hbm, guess_hbm, out,
    proj, bias_u, bias_c, w_all, w_diag, stage, mates, nears, own, packed, coefs, moves, relay_out, relay_in,
    in_sem, w_sem, mate_send, mate_recv, near_send, near_recv, coef_send, coef_recv, relay_send, relay_recv,
):
    steps, width = guess_hbm.shape
    blocks = width // BLOCK
    rows = steps * blocks
    side = 2 if blocks % 2 == 0 else 1
    group = min(GROUP, n_tm)
    n_groups = n_tm // group
    time = lax.axis_index("tm")
    unit = lax.axis_index("unit")
    place = lax.rem(time, group)
    reach = min(n_tm - 1, group if n_groups > 1 else group - 1)

    smalls = [
        pltpu.make_async_copy(source, target, in_sem.at[index])
        for index, (source, target) in enumerate((
            (guess_hbm, stage.at[0, pl.ds(0, steps)]),
            (start_hbm, stage.at[0, pl.ds(steps, 1)]),
            (proj_hbm, proj),
            (bias_u_hbm, bias_u),
            (bias_c_hbm, bias_c),
        ))
    ]
    for load in smalls:
        load.start()
    loads = [
        pltpu.make_async_copy(w_hbm.at[gate], w_all.at[gate], w_sem.at[gate]) for gate in range(3)
    ]
    for load in loads:
        load.start()

    barrier = pltpu.get_barrier_semaphore()
    greeted = jnp.int32(n_unit - 1)
    for away in range(1, n_unit):
        pl.semaphore_signal(
            barrier, inc=1, device_id=to(time, lax.rem(unit + away, n_unit)), device_id_type=MESH
        )
    for away in range(1, reach + 1):
        turns = range(n_unit if away == 1 else 1)
        for there, valid in ((time + away, time + away < n_tm), (time - away, time >= away)):
            greeted = greeted + jnp.where(valid, len(turns), 0)

            @pl.when(valid)
            def _():
                for turn in turns:
                    pl.semaphore_signal(
                        barrier, inc=1, device_id=to(there, lax.rem(unit + turn, n_unit)), device_id_type=MESH
                    )

    for load in smalls[:2]:
        load.wait()
    pl.semaphore_wait(barrier, greeted)

    def mate_copy(turn, away):
        return pltpu.make_async_remote_copy(
            src_ref=stage.at[turn], dst_ref=mates.at[turn, away - 1],
            send_sem=mate_send.at[turn, away - 1], recv_sem=mate_recv.at[turn, away - 1],
            device_id=to(time, lax.rem(unit + away, n_unit)), device_id_type=MESH,
        )

    def near_copy(away):
        return pltpu.make_async_remote_copy(
            src_ref=stage.at[0], dst_ref=nears.at[away],
            send_sem=near_send.at[away], recv_sem=near_recv.at[away],
            device_id=to(lax.rem(time + 1, n_tm), lax.rem(unit + away, n_unit)), device_id_type=MESH,
        )

    def coef_copy(turn, away):
        return pltpu.make_async_remote_copy(
            src_ref=packed.at[turn], dst_ref=coefs.at[turn, away - 1],
            send_sem=coef_send.at[turn, away - 1], recv_sem=coef_recv.at[turn, away - 1],
            device_id=to(lax.rem(time + away, n_tm), unit), device_id_type=MESH,
        )

    def relay_copy(turn, target):
        return pltpu.make_async_remote_copy(
            src_ref=relay_out.at[turn], dst_ref=relay_in.at[turn],
            send_sem=relay_send.at[turn, target], recv_sem=relay_recv.at[turn],
            device_id=to(lax.rem(time + 1 + target, n_tm), unit), device_id_type=MESH,
        )

    for away in range(1, n_unit):
        mate_copy(0, away).start()

    @pl.when(time < n_tm - 1)
    def _():
        for away in range(n_unit):
            near_copy(away).start()

    def gate_column(pair, gate):
        pairs = blocks // side
        return (2 * pair + gate if gate < 2 else 2 * pairs + pair) * BLOCK


    for load in loads:
        load.wait()
    for load in smalls[2:]:
        load.wait()
    for block in range(blocks):
        first = pl.multiple_of(unit * width + block * BLOCK, BLOCK)
        here = slice(block * BLOCK, (block + 1) * BLOCK)
        depth = block % side * BLOCK
        for gate in range(3):
            column = gate_column(block // side, gate)
            w_diag[depth : depth + BLOCK, column : column + BLOCK] = w_all[gate, pl.ds(first, BLOCK), here]

    @pl.when(time > 0)
    def _():
        for away in range(n_unit):
            near_copy(away).wait_recv()

    def entering_from(held, away):
        return jnp.where(time == 0, held[steps : steps + 1, :], nears[(n_unit - away) % n_unit, steps - 1 : steps, :])

    guess = stage[0, 0:steps, :]
    previous = jnp.concatenate([entering_from(stage[0], 0), guess[: steps - 1]], axis=0)
    row = lax.broadcasted_iota(jnp.int32, (8, BLOCK), 0)

    for turn in range(NEWTON):
        if turn:
            stage[turn, 0:steps, :] = previous
            for away in range(1, n_unit):
                mate_copy(turn, away).start()

        def product(panel, owner):
            first = pl.multiple_of(owner * width, width)
            panel = jnp.concatenate([panel] * (16 // steps), axis=0).astype(jnp.bfloat16)
            return [
                jnp.dot(panel, w_all[gate, pl.ds(first, width), :], preferred_element_type=jnp.float32)[:steps]
                for gate in range(3)
            ]

        def step(delta, five):
            left = jnp.concatenate(
                [jnp.where((row % side == depth) & (row < blocks), delta, 0.0) for depth in range(side)], axis=1
            ).astype(jnp.bfloat16)
            terms = jnp.dot(left, w_diag[...], preferred_element_type=jnp.float32)

            def of_gate(gate):
                value = None
                for pair in range(blocks // side):
                    column = gate_column(pair, gate)
                    part = terms[:, column : column + BLOCK]
                    value = part if value is None else jnp.where(row // side == pair, part, value)
                return value

            fresh, a, c, d, gap = five
            return (
                (gap + delta - fresh * delta) + a * of_gate(0) + c * of_gate(1) + d * of_gate(2)
            )

        def at_step(table, t):
            def pick(value):
                part = value[t * blocks : (t + 1) * blocks]
                return jnp.concatenate([part] * (8 // blocks), axis=0)

            return [pick(table[index]) for index in range(COEFS)]

        def pass_block(source, delta):
            away = place - source
            slot = away - 1
            pltpu.make_async_remote_copy(
                src_ref=packed.at[turn], dst_ref=coefs.at[turn, slot],
                send_sem=coef_send.at[turn, slot], recv_sem=coef_recv.at[turn, slot],
                device_id=to(lax.rem(time + 1, n_tm), unit), device_id_type=MESH,
            ).wait_recv()
            table = [coefs[turn, slot, index].astype(jnp.float32) for index in range(SENT)]
            for low, index in enumerate(FINE):
                table[index] = table[index] + table[COEFS + low]
            for t in range(steps):
                delta = step(delta, at_step(table, t))
            return delta

        rec = product(previous, unit)
        early = jnp.int32(0)
        if turn == 0:
            delta = jnp.zeros((8, BLOCK), jnp.float32)
        else:
            early = jnp.where(time < group, lax.div(2 * place, group), 0)
            delta = lax.fori_loop(0, early, pass_block, jnp.zeros((8, BLOCK), jnp.float32))
        for away in range(1, n_unit):
            mate_copy(turn, away).wait_recv()
            held = mates[turn, away - 1]
            if turn:
                panel = held[:steps]
            else:
                panel = jnp.concatenate([entering_from(held, n_unit - away), held[: steps - 1]], axis=0)
            rec = [x + y for x, y in zip(rec, product(panel, lax.rem(unit + n_unit - away, n_unit)))]

        update_in = proj[0].astype(jnp.float32) + rec[0] + bias_u[...]
        update = jax.nn.sigmoid(update_in)
        fresh = jax.nn.sigmoid(-update_in)
        reset = jax.nn.sigmoid(proj[1].astype(jnp.float32) + rec[1])
        cand_rec = rec[2] + bias_c[...]
        cand = jnp.tanh(proj[2].astype(jnp.float32) + reset * cand_rec)
        coef_d = fresh * (1.0 - cand * cand) * reset
        values = (
            fresh,
            (previous - cand) * update * fresh,
            coef_d * cand_rec * (1.0 - reset),
            coef_d,
            fresh * cand + update * previous - guess,
        )
        for index, value in enumerate(values):
            for block in range(blocks):
                own[index, pl.ds(block, steps, stride=blocks), :] = value[:, block * BLOCK : (block + 1) * BLOCK]
        packed[turn, 0:COEFS] = own[...].astype(jnp.bfloat16)
        for slot, index in enumerate(FINE):
            full = own[index]
            packed[turn, COEFS + slot] = (full - full.astype(jnp.bfloat16).astype(jnp.float32)).astype(jnp.bfloat16)

        for away in range(group - 1, 0, -1):
            @pl.when(place + away < group)
            def _():
                coef_copy(turn, away).start()

        if n_groups > 1:
            relay_in_now = relay_in.at[turn]

            @pl.when(time < group)
            def _():
                relay_in_now[...] = delta

            @pl.when(time >= group)
            def _():
                relay_copy(turn, 0).wait_recv()

            delta = relay_in_now[...]
        delta = lax.fori_loop(early, place, pass_block, delta)
        moves[0:blocks, :] = delta[:blocks]
        table = own[...]
        for t in range(steps):
            delta = step(delta, at_step(table, t))
            moves[(t + 1) * blocks : (t + 2) * blocks, :] = delta[:blocks]
        if n_groups > 1:
            relay_out[turn] = delta

            @pl.when((place == group - 1) & (time < n_tm - 1))
            def _():
                for target in reversed(range(group)):
                    relay_copy(turn, target).start()

        def moved(skip):
            return jnp.concatenate(
                [moves[pl.ds(skip * blocks + block, steps, stride=blocks), :] for block in range(blocks)], axis=1
            )

        guess = guess + moved(1)
        if turn < NEWTON - 1:
            previous = previous + moved(0)
    out[...] = guess

    @pl.when(time < n_tm - 1)
    def _():
        for away in range(n_unit):
            near_copy(away).wait_send()

    for turn in range(NEWTON):
        for away in range(1, n_unit):
            mate_copy(turn, away).wait_send()
        for away in range(1, group):
            @pl.when(place + away < group)
            def _():
                coef_copy(turn, away).wait_send()
        if n_groups > 1:
            @pl.when((place == group - 1) & (time < n_tm - 1))
            def _():
                for target in range(group):
                    relay_copy(turn, target).wait_send()


def shards(n_tm, n_unit, projections, recurrent, update_bias, candidate_bias, start_state, initial_guess):
    _, steps, _, width = projections.shape
    full = recurrent.shape[0]
    rows = steps * (width // BLOCK)
    group = min(GROUP, n_tm)
    side = 2 if width // BLOCK % 2 == 0 else 1
    vmem = pl.BlockSpec(memory_space=pltpu.VMEM)
    f32, bf16 = jnp.float32, jnp.bfloat16
    held = 8 * pl.cdiv(steps + 1, 8)
    dma = pltpu.SemaphoreType.DMA
    result = pl.pallas_call(
        functools.partial(newton_kernel, n_tm, n_unit),
        out_shape=jax.ShapeDtypeStruct((steps, width), f32),
        in_specs=[pl.BlockSpec(memory_space=pltpu.HBM)] * 6,
        out_specs=vmem,
        scratch_shapes=[
            pltpu.VMEM((3, steps, width), bf16),
            pltpu.VMEM((1, width), f32),
            pltpu.VMEM((1, width), f32),
            pltpu.VMEM((3, full, width), bf16),
            pltpu.VMEM((side * BLOCK, 3 * (width // side)), bf16),
            pltpu.VMEM((NEWTON, held, width), f32),
            pltpu.VMEM((NEWTON, n_unit - 1, held, width), f32),
            pltpu.VMEM((n_unit, held, width), f32),
            pltpu.VMEM((COEFS, rows, BLOCK), f32),
            pltpu.VMEM((NEWTON, SENT, rows, BLOCK), bf16),
            pltpu.VMEM((NEWTON, group - 1, SENT, rows, BLOCK), bf16),
            pltpu.VMEM((rows + 8, BLOCK), f32),
            pltpu.VMEM((NEWTON, 8, BLOCK), f32),
            pltpu.VMEM((NEWTON, 8, BLOCK), f32),
            dma((5,)),
            dma((3,)),
            dma((NEWTON, n_unit - 1)),
            dma((NEWTON, n_unit - 1)),
            dma((n_unit,)),
            dma((n_unit,)),
            dma((NEWTON, group - 1)),
            dma((NEWTON, group - 1)),
            dma((NEWTON, group)),
            dma((NEWTON,)),
        ],
        compiler_params=pltpu.CompilerParams(
            collective_id=0, has_side_effects=True, vmem_limit_bytes=60 * 1024 * 1024
        ),
        name="newton",
    )(
        jnp.transpose(projections[0], (1, 0, 2)),
        jnp.transpose(recurrent, (1, 0, 2)),
        update_bias.reshape(1, width),
        candidate_bias.reshape(1, width),
        start_state,
        initial_guess[0],
    )
    return result[None]


def solution(mesh):
    return jax.shard_map(
        functools.partial(shards, mesh.shape["tm"], mesh.shape["unit"]),
        mesh=mesh,
        in_specs=(
            P("sweep", "tm", None, "unit"),
            P("sweep", None, "unit"),
            P(("sweep", "unit")),
            P(("sweep", "unit")),
            P("sweep", "unit"),
            P("sweep", "tm", "unit"),
        ),
        out_specs=P("sweep", "tm", "unit"),
        check_vma=False,
    )
```
